512 devices in a mesh: cells: 32 (over y, z_lo), snd: 16 (over x, z_hi, core).
Axes of the slice: x: 4, y: 4, z: 16 (z_hi: 2, z_lo: 8; z = z_hi * 8 + z_lo), core: 2. Of those that a mesh axis runs over, the one named last changes fastest.
Arguments:
- footprint: bfloat16 [128, 4, 12288], P(None, None, ('snd', 'cells')), may hold values from -24 to 24
- spatial_cov: bfloat16 [12288, 12288], P('snd', 'cells'), as said below
- week_scale: float32 [52], replicated, may hold values from 0.5 to 2
- band_width: int32 [1], replicated, may hold values from 2 to 8
- sounding_weeks: int32 [128], replicated, may hold values from 0 to 48
- target_print: bfloat16 [4096, 4, 12288], P('snd', None, 'cells'), may hold values from -0.0546875 to 0.0546875
- target_weeks: int32 [4096], P('snd'), may hold values from 0 to 48
Outputs:
- hq_rows: bfloat16 [128, 52, 12288], P('snd', None, 'cells')
- pair_cov: float32 [128, 4096], P(None, ('snd', 'cells'))
The draws below stay inside these ranges and needn't reach their ends.
Inputs may be any that keep to these rules, and one draw needn't show every extreme that they name: spatial_cov is symmetric.
All inputs are finite; a program needn't handle non-finite values.
Results may differ from the reference program's by a relative error of at most 0.005.
Values may be sent and summed in bfloat16 or wider, within the bound.
A program may use at most 64 MiB of HBM per device.

```python
import math
import jax
import jax.numpy as jnp
from jax import lax

NC = 12288
W = 52
FOOT = 4
NS = 128
NJ = 4096


def draw_spatial_cov(key, part):
    key = jax.random.fold_in(key, 7)
    normals = jax.random.normal(key, (NC, NC), jnp.float32)
    mirrored = (normals + normals.T) * (0.5 / math.sqrt(NC))
    cell_index = jnp.arange(NC, dtype=jnp.int32)
    identity = (cell_index[:, None] == cell_index[None, :]).astype(jnp.float32)
    covariance = mirrored + 2.0 * identity
    return covariance.astype(jnp.bfloat16)


def set_ends(drawn, key, low, largest):
    spot = [jax.random.randint(jax.random.fold_in(key, axis), (), 0, length) for axis, length in enumerate(drawn.shape)]
    main_axis = drawn.shape.index(max(drawn.shape))
    beside = spot[:main_axis] + [(spot[main_axis] + 1) % drawn.shape[main_axis]] + spot[main_axis + 1:]
    return drawn.at[tuple(spot)].set(low).at[tuple(beside)].set(largest)


def strengthened(entries, rng, source, target, shards_of, factor):
    owner, partner = [(jnp.arange(entries.shape[axis_at]) // (entries.shape[axis_at] // shards_of)).reshape([-1 if axis == axis_at else 1 for axis in range(entries.ndim)]) for axis_at in (source, target)]
    chosen = jax.random.permutation(rng, shards_of)[partner]
    strong = (owner == chosen) | (owner == (partner + shards_of // 2) % shards_of)
    return jnp.where(strong, factor * entries, entries)


def level_of(stream_key, extent, cuts, low, top_value):
    def one(axis_at, shards_of):
        draws = jax.random.uniform(jax.random.fold_in(jax.random.fold_in(stream_key, 6), axis_at), (shards_of,), jnp.float32, low / len(cuts), top_value / len(cuts))
        return jnp.repeat(jnp.exp(draws), extent[axis_at] // shards_of).reshape((-1,) + (1,) * (len(extent) - axis_at - 1))

    loudness = one(*cuts[0])
    for cut in cuts[1:]:
        loudness = loudness * one(*cut)
    return loudness


def noise_with(stream_key, shape, scale, bound, pieces, heavy, kind=jnp.bfloat16):
    values = scale * jax.random.normal(stream_key, shape, jnp.float32)
    if pieces:
        values = values * level_of(stream_key, shape, pieces, -0.22, 0.18)
    return jnp.clip(strengthened(values, jax.random.fold_in(stream_key, 3), *heavy), -bound, bound).astype(kind)


def setup_inputs(seed: int = 0) -> dict:
    arg_keys = jax.random.split(jax.random.key(seed), 8)
    return {
        "footprint": noise_with(arg_keys[0], (NS, FOOT, NC), 1.0, 24.0, ((2, 512),), (2, 0, 128, 5.5)),
        "spatial_cov": draw_spatial_cov(jax.random.fold_in(arg_keys[7], 71), 0),
        "week_scale": jnp.clip(jnp.exp(jax.random.uniform(arg_keys[2], (W,), jnp.float32, math.log(0.5), math.log(2.0))), 0.5, 2.0),
        "band_width": jax.random.randint(arg_keys[3], (1,), 2, 9).astype(jnp.int32),
        "sounding_weeks": set_ends(jax.random.randint(arg_keys[4], (NS,), 0, W - 3), jax.random.fold_in(arg_keys[4], 1), 0, (W - 3) - 1).astype(jnp.int32),
        "target_print": noise_with(arg_keys[5], (NJ, FOOT, NC), (4 * NC) ** -0.5, 0.0546875, ((0, 16), (2, 32)), (2, 0, 32, 2.75)),
        "target_weeks": set_ends(jax.random.randint(arg_keys[6], (NJ,), 0, W - 3), jax.random.fold_in(arg_keys[6], 1), 0, (W - 3) - 1).astype(jnp.int32),
    }


def temporal_cov(week_scale, band_width):
    week_count = week_scale.shape[0]
    week_index = jnp.arange(week_count, dtype=jnp.int32)
    week_lag = jnp.abs(week_index[:, None] - week_index[None, :])
    in_band = (week_lag <= band_width[0]).astype(jnp.float32)
    decay = jnp.exp(-week_lag.astype(jnp.float32) / 6.0)
    return week_scale[:, None] * week_scale[None, :] * decay * in_band


def reference(footprint, spatial_cov, week_scale, band_width, sounding_weeks, target_print, target_weeks):
    table = temporal_cov(week_scale, band_width)
    sounding_count, foot_len, cell_count = footprint.shape
    target_count = target_print.shape[0]
    flux_map = jnp.dot(footprint.reshape(sounding_count * foot_len, cell_count), spatial_cov,
                       preferred_element_type=jnp.float32).astype(jnp.bfloat16)
    foot_steps = jnp.arange(foot_len, dtype=jnp.int32)
    source_week = (sounding_weeks[:, None] + foot_steps[None, :]).reshape(-1)
    target_week = (target_weeks[:, None] + foot_steps[None, :]).reshape(-1)
    spread = table[source_week].reshape(sounding_count, foot_len, -1)

    def one_sounding(pair_in):
        spread_one, flux_one = pair_in
        return jnp.dot(spread_one.T, flux_one.astype(jnp.float32),
                       precision=lax.Precision.HIGHEST).astype(jnp.bfloat16)

    hq_rows = lax.map(one_sounding, (spread, flux_map.reshape(sounding_count, foot_len, cell_count)))
    weights = table[source_week][:, target_week]
    products = lax.dot_general(flux_map, target_print.reshape(target_count * foot_len, cell_count),
                               (((1,), (1,)), ((), ())), preferred_element_type=jnp.float32)
    pair_cov = (weights * products).reshape(sounding_count, foot_len, target_count, foot_len).sum(axis=(1, 3))
    return hq_rows, pair_cov
```

```python
import functools

import jax
import jax.numpy as jnp
from jax import lax
from jax.experimental import pallas as pl
from jax.experimental.pallas import tpu as pltpu
from jax.sharding import PartitionSpec as P

MESH = pl.DeviceIdType.MESH
F32, BF16, I32 = jnp.float32, jnp.bfloat16, jnp.int32
X, Y, ZL = 4, 4, 8
CELLS, SND = 32, 16
KC = 24
COLS = 384
HALF = 256
SHARD = COLS // X
AWAY = (1, 3, 2)
BACK = (1, 0, 2)


def iota(shape, dim):
    return lax.broadcasted_iota(I32, shape, dim)


def dot_nt(a, b, precision=None):
    return lax.dot_general(
        a, b, (((1,), (1,)), ((), ())), precision=precision, preferred_element_type=F32
    )


def dot_nn(a, b, precision=None):
    return lax.dot_general(
        a, b, (((1,), (0,)), ((), ())), precision=precision, preferred_element_type=F32
    )


def flip_bits(pos, mask):
    out = 0
    for bit in (0, 1, 2):
        value = (pos // (1 << bit)) % 2
        out = out + (1 << bit) * (1 - value if mask & (1 << bit) else value)
    return out


def kernel(
    f_hbm, c_hbm, g_hbm, scale_hbm, band_ref, sw_hbm, tw_hbm,
    hq_ref, pc_ref,
    raw, c_buf, ct, g3, g2, scale_v, sw_v, tw_v,
    weights, spread, ft, acc, core_out, core_in, x_out, x_in, z_out, z_in,
    flux, pair_x, pair_out, pair_in,
    load_sem, zs_sem, zr_sem, ys_sem, yr_sem, cs_sem, cr_sem, xs_sem, xr_sem,
    hs_sem, hr_sem, gs_sem, gr_sem, fs_sem, fr_sem, ps_sem, pr_sem,
):
    cell = lax.axis_index("cells")
    snd = lax.axis_index("snd")
    x, zh, core = snd // 4, (snd // 2) % 2, snd % 2
    y, zl = cell // ZL, cell % ZL

    def at_cells(yy, zz):
        return (yy * ZL + zz, snd)

    def at_snd(xx, hh, cc):
        return (cell, (xx * 2 + hh) * 2 + cc)

    def remote(src, dst, send, recv, device):
        return pltpu.make_async_remote_copy(
            src_ref=src, dst_ref=dst, send_sem=send, recv_sem=recv,
            device_id=device, device_id_type=MESH,
        )

    z_peers = [flip_bits(zl, m) for m in range(1, ZL)]
    y_peers = [(y + d) % Y for d in AWAY]
    x_peers = [(x + d) % X for d in AWAY]
    opposite = at_snd(x, 1 - zh, core)
    sibling = at_snd(x, zh, 1 - core)

    barrier = pltpu.get_barrier_semaphore()
    greeted = [opposite]
    greeted += [at_cells(y, p) for p in z_peers[::-1]]
    greeted += [at_cells(p, zl) for p in y_peers]
    greeted += [at_snd(p, zh, core) for p in x_peers]
    greeted += [sibling]
    for device in greeted:
        pl.semaphore_signal(barrier, inc=1, device_id=device, device_id_type=MESH)

    load_f = pltpu.make_async_copy(f_hbm, raw.at[cell], load_sem.at[0])
    load_f.start()
    loads = [
        pltpu.make_async_copy(src, dst, load_sem.at[1 + n])
        for n, (src, dst) in enumerate(
            ((scale_hbm, scale_v), (sw_hbm, sw_v), (tw_hbm, tw_v), (c_hbm, c_buf), (g_hbm, g3))
        )
    ]
    for copy in loads:
        copy.start()
    load_f.wait()
    pl.semaphore_wait(barrier, len(greeted))

    for m, peer in enumerate(z_peers):
        remote(raw.at[cell], raw.at[cell], zs_sem, zr_sem.at[m], at_cells(y, peer)).start()
    for n, peer in enumerate(y_peers):
        remote(raw.at[cell], raw.at[cell], ys_sem, yr_sem.at[BACK[n]], at_cells(peer, zl)).start()

    def forward(m):
        block = raw.at[y * ZL + z_peers[m]]
        remote(block, block, zs_sem, zr_sem.at[m], opposite).wait_recv()
        for n, peer in enumerate(y_peers):
            remote(block, block, ys_sem, yr_sem.at[BACK[n]], at_cells(peer, zl)).start()

    for copy in loads[:3]:
        copy.wait()
    top = lax.Precision.HIGHEST
    scale8 = jnp.broadcast_to(scale_v[...], (8, 52))
    eye = (iota((64, 52), 0) == iota((64, 52), 1)).astype(F32)
    scale_row = dot_nt(scale8, eye, top)
    scale_col = dot_nt(eye, scale8, top)
    lag = jnp.abs(iota((64, 64), 0) - iota((64, 64), 1))
    decay = jnp.exp(lag.astype(F32) * (-1.0 / 6.0))
    table = jnp.where(lag <= band_ref[0], decay, 0.0)
    table = table * scale_col[:, 0:1] * scale_row[0:1, :]
    first = sw_v[...]
    weeks = jnp.concatenate([first + a for a in range(4)], axis=1)
    source_pick = (iota((64, 512), 0) == weeks).astype(F32)
    source_rows = dot_nn(table, source_pick, top)
    row_hi = source_rows.astype(BF16)
    rest = source_rows - row_hi.astype(F32)
    row_mid = rest.astype(BF16)
    row_lo = (rest - row_mid.astype(F32)).astype(BF16)
    rows3 = jnp.concatenate([row_hi, row_mid, row_lo], axis=0)
    repeat = ((iota((1024, 256), 0) >> 2) == iota((1024, 256), 1)).astype(BF16)
    target_first = jnp.broadcast_to(tw_v[...], (8, 256)).astype(F32).astype(BF16)
    target_col = dot_nt(repeat, target_first)[:, 0:1].astype(I32)
    target_week = target_col + (iota((1024, 1), 0) & 3)
    target_pick = ((iota((1024, 192), 1) & 63) == target_week).astype(F32).astype(BF16)
    forward(0)
    for h in range(2):
        weights[h] = dot_nn(target_pick, rows3[:, h * HALF : (h + 1) * HALF])
    forward(1)
    forward(2)
    mine = (iota((8, 512), 1) & 127) == iota((8, 512), 0) + snd * 8
    mine = mine.astype(F32)
    wide = (source_rows[:52].reshape(52, 1, 512) * mine.reshape(1, 8, 512)).reshape(416, 512)
    wide_hi = wide.astype(BF16)
    wide_lo = (wide - wide_hi.astype(F32)).astype(BF16)
    for h in range(2):
        spread[0, h] = wide_hi[:, h * HALF : (h + 1) * HALF]
        spread[1, h] = wide_lo[:, h * HALF : (h + 1) * HALF]
    forward(3)
    loads[3].wait()
    for q in range(Y):
        rows = KC * ZL
        ct[q] = c_buf[q * rows : (q + 1) * rows, :].astype(F32).T.astype(BF16)
    forward(4)
    forward(5)
    forward(6)
    loads[4].wait()
    g2[...] = g3[...].reshape(1024, COLS)

    def unpack(yy):
        blocks = raw[pl.ds(yy * ZL, ZL)].astype(F32)
        for a in range(4):
            part = blocks[:, a * KC : (a + 1) * KC, :].reshape(ZL * KC, 128).astype(BF16)
            ft[a // 2, :, (a % 2) * 128 : (a % 2 + 1) * 128] = part

    unpack(y)
    for h in range(2):
        acc[h] = dot_nn(ct[y], ft[h])
    for n, peer in enumerate(y_peers):
        part = raw.at[pl.ds(peer * ZL, ZL)]
        remote(part, part, ys_sem, yr_sem.at[n], opposite).wait_recv()
        unpack(peer)
        if n < 2:
            for h in range(2):
                acc[h] += dot_nn(ct[peer], ft[h])
        else:
            core_out[...] = (acc[1 - core] + dot_nn(ct[peer], ft[1 - core])).astype(BF16)
            to_core = remote(core_out, core_in, cs_sem, cr_sem, sibling)
            to_core.start()
            acc[core] += dot_nn(ct[peer], ft[core])

    to_core.wait_recv()
    chip_sum = acc[core] + core_in[...].astype(F32)
    acc[core] = chip_sum
    x_out[...] = chip_sum.astype(BF16).reshape(X, SHARD, HALF)
    x_copies = []
    for n, peer in enumerate(x_peers):
        copy = remote(x_out.at[peer], x_in.at[n], xs_sem, xr_sem, at_snd(peer, zh, core))
        copy.start()
        x_copies.append(copy)
    own = acc[core, pl.ds(pl.multiple_of(x * SHARD, SHARD), SHARD), :]
    remote(x_in, x_in, xs_sem, xr_sem, opposite).wait_recv()
    own = own + (x_in[0].astype(F32) + x_in[1].astype(F32) + x_in[2].astype(F32))
    z_out[...] = own.astype(BF16)
    to_z = remote(z_out, z_in, hs_sem, hr_sem, opposite)
    to_z.start()
    to_z.wait_recv()
    flux[core, x] = (own + z_in[...].astype(F32)).astype(BF16)

    def share(n, peer):
        block = flux.at[core, peer]
        remote(block, block, fs_sem, fr_sem, sibling).start()

    shard = flux.at[core, x]
    for n, peer in enumerate(x_peers):
        remote(shard, shard, gs_sem, gr_sem.at[BACK[n]], at_snd(peer, zh, core)).start()
    share(3, x)
    for n, peer in enumerate(x_peers):
        block = flux.at[core, peer]
        remote(block, block, gs_sem, gr_sem.at[n], opposite).wait_recv()
        share(n, peer)

    def products(h):
        both = dot_nn(g2[...], flux[h].reshape(COLS, HALF)) * weights[h]
        return both[:, :128] + both[:, 128:]

    pair_x[...] = products(core)
    whole = flux.at[1 - core]
    remote(whole, whole, fs_sem, fr_sem, sibling).wait_recv()
    total = pair_x[...] + products(1 - core)
    gather = ((iota((256, 1024), 1) >> 2) == iota((256, 1024), 0)).astype(BF16)
    total_hi = total.astype(BF16)
    total_lo = (total - total_hi.astype(F32)).astype(BF16)
    pair = dot_nn(gather, total_hi) + dot_nn(gather, total_lo)
    pair_out[...] = pair.reshape(CELLS, 8, 128)

    def send_pair(o, carry):
        target = (cell + o) % CELLS
        remote(
            pair_out.at[target], pair_in.at[o - 1], ps_sem, pr_sem, (target, snd)
        ).start()
        return carry

    lax.fori_loop(1, CELLS, send_pair, 0)

    hq = jnp.zeros((416, COLS), F32)
    for h in range(2):
        columns = flux[h].reshape(COLS, HALF)
        hq = hq + dot_nt(spread[0, h], columns) + dot_nt(spread[1, h], columns)
    hq_ref[...] = hq.astype(BF16)

    remote(pair_in, pair_in, ps_sem, pr_sem, opposite).wait_recv()
    pc_ref[...] = pair_out[cell] + jnp.sum(pair_in[...], axis=0)

    sent = raw.at[pl.ds(0, ZL - 1)]
    remote(sent, sent, zs_sem, zr_sem.at[0], opposite).wait_send()
    sent = raw.at[pl.ds(0, ZL * (Y - 1))]
    remote(sent, sent, ys_sem, yr_sem.at[0], opposite).wait_send()
    to_core.wait_send()
    remote(x_in, x_in, xs_sem, xr_sem, opposite).wait_send()
    to_z.wait_send()
    remote(x_in, x_in, gs_sem, gr_sem.at[0], opposite).wait_send()
    remote(x_out, x_out, fs_sem, fr_sem, sibling).wait_send()
    remote(pair_in, pair_in, ps_sem, pr_sem, opposite).wait_send()


def shards(
    footprint, spatial_cov, week_scale, band_width, sounding_weeks, target_print, target_weeks
):
    any_spec = pl.BlockSpec(memory_space=pl.ANY)
    vmem = pl.BlockSpec(memory_space=pltpu.VMEM)
    dma = pltpu.SemaphoreType.DMA
    hq, pair = pl.pallas_call(
        kernel,
        out_shape=(
            jax.ShapeDtypeStruct((416, COLS), BF16),
            jax.ShapeDtypeStruct((8, 128), F32),
        ),
        in_specs=[any_spec] * 4 + [pl.BlockSpec(memory_space=pltpu.SMEM)] + [any_spec] * 2,
        out_specs=(vmem, vmem),
        scratch_shapes=[
            pltpu.VMEM((CELLS, 4 * KC, 128), BF16),
            pltpu.VMEM((768, COLS), BF16),
            pltpu.VMEM((Y, COLS, KC * ZL), BF16),
            pltpu.VMEM((256, 4, COLS), BF16),
            pltpu.VMEM((1024, COLS), BF16),
            pltpu.VMEM((1, 52), F32),
            pltpu.VMEM((1, 128), I32),
            pltpu.VMEM((1, 256), I32),
            pltpu.VMEM((2, 1024, HALF), F32),
            pltpu.VMEM((2, 2, 416, HALF), BF16),
            pltpu.VMEM((2, KC * ZL, HALF), BF16),
            pltpu.VMEM((2, COLS, HALF), F32),
            pltpu.VMEM((COLS, HALF), BF16),
            pltpu.VMEM((COLS, HALF), BF16),
            pltpu.VMEM((X, SHARD, HALF), BF16),
            pltpu.VMEM((X - 1, SHARD, HALF), BF16),
            pltpu.VMEM((SHARD, HALF), BF16),
            pltpu.VMEM((SHARD, HALF), BF16),
            pltpu.VMEM((2, X, SHARD, HALF), BF16),
            pltpu.VMEM((1024, 128), F32),
            pltpu.VMEM((CELLS, 8, 128), F32),
            pltpu.VMEM((CELLS - 1, 8, 128), F32),
            dma((6,)),
            dma, dma((ZL - 1,)),
            dma, dma((Y - 1,)),
            dma, dma,
            dma, dma,
            dma, dma,
            dma, dma((X - 1,)),
            dma, dma,
            dma, dma,
        ],
        compiler_params=pltpu.CompilerParams(
            collective_id=0, has_side_effects=True, vmem_limit_bytes=48 << 20
        ),
        name="prior_products",
    )(
        jnp.transpose(footprint, (1, 2, 0)).reshape(4 * KC, 128),
        spatial_cov,
        target_print,
        week_scale.reshape(1, 52),
        band_width,
        sounding_weeks.reshape(1, 128),
        target_weeks.reshape(1, 256),
    )
    return jnp.transpose(hq.reshape(52, 8, COLS), (1, 0, 2)), pair.T


def solution(mesh):
    placed = (
        P(None, None, ("snd", "cells")),
        P("snd", "cells"),
        P(),
        P(),
        P(),
        P("snd", None, "cells"),
        P("snd"),
    )
    return jax.shard_map(
        shards,
        mesh=mesh,
        in_specs=placed,
        out_specs=(P("snd", None, "cells"), P(None, ("snd", "cells"))),
        check_vma=False,
    )
```

```python
import jax
import jax.numpy as jnp
from jax import lax
from jax.experimental import pallas as pl
from jax.experimental.pallas import tpu as pltpu
from jax.sharding import PartitionSpec as P

MESH = pl.DeviceIdType.MESH
F32, BF16, I32 = jnp.float32, jnp.bfloat16, jnp.int32
X, Y, ZL = 4, 4, 8
CELLS, SND = 32, 16
KC = 24
COLS = 384
HALF = 256
SHARD = COLS // X
AWAY = (1, 3, 2)
BACK = (1, 0, 2)


def iota(shape, dim):
    return lax.broadcasted_iota(I32, shape, dim)


def dot_nt(a, b, precision=None):
    return lax.dot_general(
        a, b, (((1,), (1,)), ((), ())), precision=precision, preferred_element_type=F32
    )


def dot_nn(a, b, precision=None):
    return lax.dot_general(
        a, b, (((1,), (0,)), ((), ())), precision=precision, preferred_element_type=F32
    )


def flip_bits(pos, mask):
    out = 0
    for bit in (0, 1, 2):
        value = (pos // (1 << bit)) % 2
        out = out + (1 << bit) * (1 - value if mask & (1 << bit) else value)
    return out


def kernel(
    f_hbm, c_hbm, g_hbm, scale_hbm, band_ref, sw_hbm, tw_hbm,
    hq_ref, pc_ref,
    raw, c_buf, ct, g3, g2, scale_v, sw_v, tw_v,
    weights, spread, ft, acc, core_out, core_in, x_out, x_in, z_out, z_in,
    flux, pair_x, pair_out, pair_in,
    load_sem, zs_sem, zr_sem, ys_sem, yr_sem, cs_sem, cr_sem, xs_sem, xr_sem,
    hs_sem, hr_sem, gs_sem, gr_sem, fs_sem, fr_sem, ps_sem, pr_sem,
):
    cell = lax.axis_index("cells")
    snd = lax.axis_index("snd")
    x, zh, core = snd // 4, (snd // 2) % 2, snd % 2
    y, zl = cell // ZL, cell % ZL

    def at_cells(yy, zz):
        return (yy * ZL + zz, snd)

    def at_snd(xx, hh, cc):
        return (cell, (xx * 2 + hh) * 2 + cc)

    def remote(src, dst, send, recv, device):
        return pltpu.make_async_remote_copy(
            src_ref=src, dst_ref=dst, send_sem=send, recv_sem=recv,
            device_id=device, device_id_type=MESH,
        )

    drains = []

    def finish():
        for drain in drains:
            drain()

    def later(ref, sem):
        drains.append(remote(ref, ref, sem, load_sem.at[0], (cell, 15 - snd)).wait_send)

    z_peers = [flip_bits(zl, m) for m in range(1, ZL)]
    y_peers = [(y + d) % Y for d in AWAY]
    x_peers = [(x + d) % X for d in AWAY]
    opposite = at_snd(x, 1 - zh, core)
    sibling = at_snd(x, zh, 1 - core)

    barrier = pltpu.get_barrier_semaphore()
    greeted = [opposite]
    greeted += [at_cells(y, p) for p in z_peers[::-1]]
    greeted += [at_cells(p, zl) for p in y_peers]
    greeted += [at_snd(p, zh, core) for p in x_peers]
    greeted += [sibling]
    for device in greeted:
        pl.semaphore_signal(barrier, inc=1, device_id=device, device_id_type=MESH)

    load_f = pltpu.make_async_copy(f_hbm, raw.at[cell], load_sem.at[0])
    load_f.start()
    loads = [
        pltpu.make_async_copy(src, dst, load_sem.at[1 + n])
        for n, (src, dst) in enumerate(
            ((scale_hbm, scale_v), (sw_hbm, sw_v), (tw_hbm, tw_v), (c_hbm, c_buf), (g_hbm, g3))
        )
    ]
    for copy in loads:
        copy.start()
    for copy in loads[:3]:
        copy.wait()
    top = lax.Precision.HIGHEST
    scale8 = jnp.broadcast_to(scale_v[...], (8, 52))
    eye = (iota((64, 52), 0) == iota((64, 52), 1)).astype(F32)
    scale_row = dot_nt(scale8, eye, top)
    scale_col = dot_nt(eye, scale8, top)
    lag = jnp.abs(iota((64, 64), 0) - iota((64, 64), 1))
    decay = jnp.exp(lag.astype(F32) * (-1.0 / 6.0))
    table = jnp.where(lag <= band_ref[0], decay, 0.0)
    table = table * scale_col[:, 0:1] * scale_row[0:1, :]
    first = sw_v[...]
    weeks = jnp.concatenate([first + a for a in range(4)], axis=1)
    source_pick = (iota((64, 512), 0) == weeks).astype(F32)
    source_rows = dot_nn(table, source_pick, top)
    row_hi = source_rows.astype(BF16)
    rest = source_rows - row_hi.astype(F32)
    row_mid = rest.astype(BF16)
    row_lo = (rest - row_mid.astype(F32)).astype(BF16)
    rows3 = jnp.concatenate([row_hi, row_mid, row_lo], axis=0)
    repeat = ((iota((1024, 256), 0) >> 2) == iota((1024, 256), 1)).astype(BF16)
    target_first = jnp.broadcast_to(tw_v[...], (8, 256)).astype(F32).astype(BF16)
    target_col = dot_nt(repeat, target_first)[:, 0:1].astype(I32)
    target_week = target_col + (iota((1024, 1), 0) & 3)
    target_pick = ((iota((1024, 192), 1) & 63) == target_week).astype(F32).astype(BF16)
    for h in range(2):
        weights[h] = dot_nn(target_pick, rows3[:, h * HALF : (h + 1) * HALF])
    loads[3].wait()
    for q in range(Y):
        rows = KC * ZL
        ct[q] = c_buf[q * rows : (q + 1) * rows, :].astype(F32).T.astype(BF16)
    load_f.wait()
    pl.semaphore_wait(barrier, len(greeted))

    later(raw.at[pl.ds(0, ZL - 1)], zs_sem)
    later(raw.at[pl.ds(0, ZL * (Y - 1))], ys_sem)
    for m, peer in enumerate(z_peers):
        remote(raw.at[cell], raw.at[cell], zs_sem, zr_sem.at[m], at_cells(y, peer)).start()
    for n, peer in enumerate(y_peers):
        remote(raw.at[cell], raw.at[cell], ys_sem, yr_sem.at[BACK[n]], at_cells(peer, zl)).start()

    def forward(m):
        block = raw.at[y * ZL + z_peers[m]]
        remote(block, block, zs_sem, zr_sem.at[m], opposite).wait_recv()
        for n, peer in enumerate(y_peers):
            remote(block, block, ys_sem, yr_sem.at[BACK[n]], at_cells(peer, zl)).start()

    forward(0)
    forward(1)
    forward(2)
    forward(3)
    forward(4)
    forward(5)
    forward(6)
    mine = (iota((8, 512), 1) & 127) == iota((8, 512), 0) + snd * 8
    mine = mine.astype(F32)
    wide = (source_rows[:52].reshape(52, 1, 512) * mine.reshape(1, 8, 512)).reshape(416, 512)
    wide_hi = wide.astype(BF16)
    wide_lo = (wide - wide_hi.astype(F32)).astype(BF16)
    for h in range(2):
        spread[0, h] = wide_hi[:, h * HALF : (h + 1) * HALF]
        spread[1, h] = wide_lo[:, h * HALF : (h + 1) * HALF]
    loads[4].wait()
    g2[...] = g3[...].reshape(1024, COLS)


    def unpack(yy):
        blocks = raw[pl.ds(yy * ZL, ZL)].astype(F32)
        for a in range(4):
            part = blocks[:, a * KC : (a + 1) * KC, :].reshape(ZL * KC, 128).astype(BF16)
            ft[a // 2, :, (a % 2) * 128 : (a % 2 + 1) * 128] = part

    unpack(y)
    for h in range(2):
        acc[h] = dot_nn(ct[y], ft[h])
    for n, peer in enumerate(y_peers):
        part = raw.at[pl.ds(peer * ZL, ZL)]
        remote(part, part, ys_sem, yr_sem.at[n], opposite).wait_recv()
        unpack(peer)
        if n < 2:
            for h in range(2):
                acc[h] += dot_nn(ct[peer], ft[h])
        else:
            core_out[...] = (acc[1 - core] + dot_nn(ct[peer], ft[1 - core])).astype(BF16)
            to_core = remote(core_out, core_in, cs_sem, cr_sem, sibling)
            to_core.start()
            acc[core] += dot_nn(ct[peer], ft[core])

    drains.append(to_core.wait_send)
    to_core.wait_recv()
    chip_sum = acc[core] + core_in[...].astype(F32)
    acc[core] = chip_sum
    x_out[...] = chip_sum.astype(BF16).reshape(X, SHARD, HALF)
    later(x_in, xs_sem)
    for n, peer in enumerate(x_peers):
        remote(x_out.at[peer], x_in.at[n], xs_sem, xr_sem, at_snd(peer, zh, core)).start()
    own = acc[core, pl.ds(pl.multiple_of(x * SHARD, SHARD), SHARD), :]
    remote(x_in, x_in, xs_sem, xr_sem, opposite).wait_recv()
    own = own + (x_in[0].astype(F32) + x_in[1].astype(F32) + x_in[2].astype(F32))
    z_out[...] = own.astype(BF16)
    to_z = remote(z_out, z_in, hs_sem, hr_sem, opposite)
    to_z.start()
    drains.append(to_z.wait_send)
    to_z.wait_recv()
    flux[core, x] = (own + z_in[...].astype(F32)).astype(BF16)

    def share(n, peer):
        block = flux.at[core, peer]
        remote(block, block, fs_sem, fr_sem, sibling).start()

    shard = flux.at[core, x]
    later(x_in, gs_sem)
    later(x_out, fs_sem)
    for n, peer in enumerate(x_peers):
        remote(shard, shard, gs_sem, gr_sem.at[BACK[n]], at_snd(peer, zh, core)).start()
    share(3, x)
    for n, peer in enumerate(x_peers):
        block = flux.at[core, peer]
        remote(block, block, gs_sem, gr_sem.at[n], opposite).wait_recv()
        share(n, peer)

    def products(h):
        both = dot_nn(g2[...], flux[h].reshape(COLS, HALF)) * weights[h]
        return both[:, :128] + both[:, 128:]

    pair_x[...] = products(core)
    whole = flux.at[1 - core]
    remote(whole, whole, fs_sem, fr_sem, sibling).wait_recv()
    total = pair_x[...] + products(1 - core)
    gather = ((iota((256, 1024), 1) >> 2) == iota((256, 1024), 0)).astype(BF16)
    total_hi = total.astype(BF16)
    total_lo = (total - total_hi.astype(F32)).astype(BF16)
    pair = dot_nn(gather, total_hi) + dot_nn(gather, total_lo)
    pair_out[...] = pair.reshape(CELLS, 8, 128)

    later(pair_in, ps_sem)
    for m in range(ZL - 1, -1, -1):
        for d in (2, 1, 3, 0):
            if m or d:
                target = ((y + d) % Y) * ZL + (z_peers[m - 1] if m else zl)
                remote(
                    pair_out.at[target], pair_in.at[m * Y + d - 1], ps_sem, pr_sem, (target, snd)
                ).start()

    hq = jnp.zeros((416, COLS), F32)
    for h in range(2):
        columns = flux[h].reshape(COLS, HALF)
        hq = hq + dot_nt(spread[0, h], columns) + dot_nt(spread[1, h], columns)
    hq_ref[...] = hq.astype(BF16)

    remote(pair_in, pair_in, ps_sem, pr_sem, opposite).wait_recv()
    pc_ref[...] = pair_out[cell] + jnp.sum(pair_in[...], axis=0)

    finish()


def shards(
    footprint, spatial_cov, week_scale, band_width, sounding_weeks, target_print, target_weeks,
):
    any_spec = pl.BlockSpec(memory_space=pl.ANY)
    vmem = pl.BlockSpec(memory_space=pltpu.VMEM)
    dma = pltpu.SemaphoreType.DMA
    hq, pair = pl.pallas_call(
        kernel,
        out_shape=(
            jax.ShapeDtypeStruct((416, COLS), BF16),
            jax.ShapeDtypeStruct((8, 128), F32),
        ),
        in_specs=[any_spec] * 4 + [pl.BlockSpec(memory_space=pltpu.SMEM)] + [any_spec] * 2,
        out_specs=(vmem, vmem),
        scratch_shapes=[
            pltpu.VMEM((CELLS, 4 * KC, 128), BF16),
            pltpu.VMEM((768, COLS), BF16),
            pltpu.VMEM((Y, COLS, KC * ZL), BF16),
            pltpu.VMEM((256, 4, COLS), BF16),
            pltpu.VMEM((1024, COLS), BF16),
            pltpu.VMEM((1, 52), F32),
            pltpu.VMEM((1, 128), I32),
            pltpu.VMEM((1, 256), I32),
            pltpu.VMEM((2, 1024, HALF), F32),
            pltpu.VMEM((2, 2, 416, HALF), BF16),
            pltpu.VMEM((2, KC * ZL, HALF), BF16),
            pltpu.VMEM((2, COLS, HALF), F32),
            pltpu.VMEM((COLS, HALF), BF16),
            pltpu.VMEM((COLS, HALF), BF16),
            pltpu.VMEM((X, SHARD, HALF), BF16),
            pltpu.VMEM((X - 1, SHARD, HALF), BF16),
            pltpu.VMEM((SHARD, HALF), BF16),
            pltpu.VMEM((SHARD, HALF), BF16),
            pltpu.VMEM((2, X, SHARD, HALF), BF16),
            pltpu.VMEM((1024, 128), F32),
            pltpu.VMEM((CELLS, 8, 128), F32),
            pltpu.VMEM((CELLS - 1, 8, 128), F32),
            dma((6,)),
            dma, dma((ZL - 1,)),
            dma, dma((Y - 1,)),
            dma, dma,
            dma, dma,
            dma, dma,
            dma, dma((X - 1,)),
            dma, dma,
            dma, dma,
        ],
        compiler_params=pltpu.CompilerParams(
            collective_id=0, has_side_effects=True, vmem_limit_bytes=62 << 20
        ),
        name="prior_products",
    )(
        jnp.transpose(footprint, (1, 2, 0)).reshape(4 * KC, 128),
        spatial_cov,
        target_print,
        week_scale.reshape(1, 52),
        band_width,
        sounding_weeks.reshape(1, 128),
        target_weeks.reshape(1, 256),
    )
    return jnp.transpose(hq.reshape(52, 8, COLS), (1, 0, 2)), pair.T


def solution(mesh):
    placed = (
        P(None, None, ("snd", "cells")),
        P("snd", "cells"),
        P(),
        P(),
        P(),
        P("snd", None, "cells"),
        P("snd"),
    )
    return jax.shard_map(
        shards,
        mesh=mesh,
        in_specs=placed,
        out_specs=(P("snd", None, "cells"), P(None, ("snd", "cells"))),
        check_vma=False,
    )
```

```python
import jax
import jax.numpy as jnp
from jax import lax
from jax.experimental import pallas as pl
from jax.experimental.pallas import tpu as pltpu
from jax.sharding import PartitionSpec as P

MESH = pl.DeviceIdType.MESH
F32, BF16, I32 = jnp.float32, jnp.bfloat16, jnp.int32
X, Y, ZL = 4, 4, 8
CELLS = 32
KC = 24
COLS = 384
SHARD = COLS // X
CHUNKS = 2
ROWS = 2 * KC
GROUP = ZL * KC
AWAY = (1, 3, 2)
BACK = (1, 0, 2)
FAR_FIRST = (7, 6, 5, 4, 3, 2, 1)
NEAR_FIRST = (1, 2, 3, 4, 5, 6, 7)


def iota(shape, dim):
    return lax.broadcasted_iota(I32, shape, dim)


def dot_nt(a, b, precision=None):
    return lax.dot_general(
        a, b, (((1,), (1,)), ((), ())), precision=precision, preferred_element_type=F32
    )


def dot_nn(a, b, precision=None):
    return lax.dot_general(
        a, b, (((1,), (0,)), ((), ())), precision=precision, preferred_element_type=F32
    )


def flip_bits(pos, mask):
    out = 0
    for bit in (0, 1, 2):
        value = (pos // (1 << bit)) % 2
        out = out + (1 << bit) * (1 - value if mask & (1 << bit) else value)
    return out


def in_hbm(array):
    return pltpu.with_memory_space_constraint(array, pltpu.HBM)


def kernel(
    f_hbm, c_hbm, g_hbm, scale_hbm, band_ref, sw_hbm, tw_hbm,
    hq_ref, pc_ref,
    raw, c_buf, ct, g3, g2, scale_v, sw_v, tw_v,
    weights, spread, acc, sum_out, sum_in, z_out, z_in, z_own,
    flux, pair_x, pair_out, pair_in,
    load_sem, zs_sem, zr_sem, ys_sem, yr_sem, ss_sem, sr_sem,
    hs_sem, hr_sem, gs_sem, gr_sem, ps_sem, pr_sem, token,
):
    cell = lax.axis_index("cells")
    snd = lax.axis_index("snd")
    x, zh, core = snd // 4, (snd // 2) % 2, snd % 2
    y, zl = cell // ZL, cell % ZL

    def at_cells(yy, zz):
        return (yy * ZL + zz, snd)

    def at_snd(xx, hh, cc):
        return (cell, (xx * 2 + hh) * 2 + cc)

    def remote(src, dst, send, recv, device):
        return pltpu.make_async_remote_copy(
            src_ref=src, dst_ref=dst, send_sem=send, recv_sem=recv,
            device_id=device, device_id_type=MESH,
        )

    drains = []

    def finish():
        for drain in drains:
            drain()

    def later(ref, sem):
        drains.append(remote(ref, ref, sem, load_sem.at[0], opposite).wait_send)

    z_peer = {m: flip_bits(zl, m) for m in NEAR_FIRST}
    y_peers = [(y + d) % Y for d in AWAY]
    sum_peers = [
        ((x + d) % X, (core + f) % 2) for d in (2, 1, 3, 0) for f in (0, 1) if d or f
    ]
    opposite = at_snd(x, 1 - zh, core)
    across = (y * ZL + z_peer[4], (x * 2 + 1 - zh) * 2 + core)

    barrier = pltpu.get_barrier_semaphore()
    greeted = [at_cells(y, z_peer[m]) for m in FAR_FIRST] + [across]
    greeted += [at_cells(p, zl) for p in y_peers]
    greeted += [at_snd(xx, zh, cc) for xx, cc in sum_peers]
    for device in greeted:
        pl.semaphore_signal(barrier, inc=1, device_id=device, device_id_type=MESH)

    load_f = pltpu.make_async_copy(f_hbm, raw.at[cell], load_sem.at[0])
    load_f.start()
    loads = [
        pltpu.make_async_copy(src, dst, load_sem.at[1 + n])
        for n, (src, dst) in enumerate(
            ((scale_hbm, scale_v), (sw_hbm, sw_v), (tw_hbm, tw_v), (c_hbm, c_buf), (g_hbm, g3))
        )
    ]
    for copy in loads:
        copy.start()

    for copy in loads[:3]:
        copy.wait()
    top = lax.Precision.HIGHEST
    scale8 = jnp.broadcast_to(scale_v[...], (8, 52))
    eye = (iota((64, 52), 0) == iota((64, 52), 1)).astype(F32)
    scale_row = dot_nt(scale8, eye, top)
    scale_col = dot_nt(eye, scale8, top)
    lag = jnp.abs(iota((64, 64), 0) - iota((64, 64), 1))
    decay = jnp.exp(lag.astype(F32) * (-1.0 / 6.0))
    table = jnp.where(lag <= band_ref[0], decay, 0.0)
    table = table * scale_col[:, 0:1] * scale_row[0:1, :]
    first = sw_v[...]
    weeks = jnp.concatenate([first + a for a in range(4)], axis=1)
    source_pick = (iota((64, 512), 0) == weeks).astype(F32)
    source_rows = dot_nn(table, source_pick, top)
    row_hi = source_rows.astype(BF16)
    rest = source_rows - row_hi.astype(F32)
    row_mid = rest.astype(BF16)
    row_lo = (rest - row_mid.astype(F32)).astype(BF16)
    rows3 = jnp.concatenate([row_hi, row_mid, row_lo], axis=0)
    repeat = ((iota((1024, 256), 0) >> 2) == iota((1024, 256), 1)).astype(BF16)
    target_first = jnp.broadcast_to(tw_v[...], (8, 256)).astype(F32).astype(BF16)
    target_col = dot_nt(repeat, target_first)[:, 0:1].astype(I32)
    target_week = target_col + (iota((1024, 1), 0) & 3)
    target_pick = ((iota((1024, 192), 1) & 63) == target_week).astype(F32).astype(BF16)
    for q in range(CHUNKS):
        weights[q] = dot_nn(target_pick, rows3[:, q * 256 : (q + 1) * 256])
    loads[3].wait()
    for g in range(Y):
        ct[g] = c_buf[g * GROUP : (g + 1) * GROUP, :].astype(F32).T.astype(BF16)

    load_f.wait()
    pl.semaphore_wait(barrier, len(greeted))
    pl.semaphore_signal(token, inc=1, device_id=across, device_id_type=MESH)

    later(raw.at[pl.ds(0, ZL - 1)], zs_sem)
    later(raw.at[pl.ds(0, ZL * (Y - 1))], ys_sem)

    def piece(q, block):
        return raw.at[block, pl.ds(q * ROWS, ROWS)]

    def along_y(q, block):
        part = piece(q, block)
        for n, peer in enumerate(y_peers):
            remote(part, part, ys_sem, yr_sem.at[q, BACK[n]], at_cells(peer, zl)).start()

    for q in range(CHUNKS):
        part = piece(q, cell)
        for m in NEAR_FIRST:
            remote(
                part, part, zs_sem, zr_sem.at[q, m - 1], at_cells(y, z_peer[m])
            ).start()
        along_y(q, cell)
    for q in range(CHUNKS):
        for m in NEAR_FIRST:
            block = y * ZL + z_peer[m]
            part = piece(q, block)
            remote(part, part, zs_sem, zr_sem.at[q, m - 1], opposite).wait_recv()
            along_y(q, block)

    loads[4].wait()
    g2[...] = g3[...].reshape(1024, COLS)
    mine = (iota((8, 512), 1) & 127) == iota((8, 512), 0) + snd * 8
    mine = mine.astype(F32)
    wide = (source_rows[:52].reshape(52, 1, 512) * mine.reshape(1, 8, 512)).reshape(416, 512)
    wide_hi = wide.astype(BF16)
    wide_lo = (wide - wide_hi.astype(F32)).astype(BF16)
    for q in range(CHUNKS):
        spread[0, q] = wide_hi[:, q * 256 : (q + 1) * 256]
        spread[1, q] = wide_lo[:, q * 256 : (q + 1) * 256]

    def unpack(q, group):
        blocks = raw[pl.ds(group * ZL, ZL), q * ROWS : (q + 1) * ROWS].astype(F32)
        return jnp.concatenate(
            [
                blocks[:, a * KC : (a + 1) * KC, :].reshape(GROUP, 128).astype(BF16)
                for a in range(2)
            ],
            axis=1,
        )

    def partial_flux(q):
        total = dot_nn(ct[y], unpack(q, y))
        for n, peer in enumerate(y_peers):
            part = raw.at[pl.ds(peer * ZL, ZL), pl.ds(q * ROWS, ROWS)]
            remote(part, part, ys_sem, yr_sem.at[q, n], opposite).wait_recv()
            total = total + dot_nn(ct[peer], unpack(q, peer))
        for c in range(2):
            half = total[:, c * 128 : (c + 1) * 128]
            acc[q, c] = half
            sum_out[q, c] = half.astype(BF16).reshape(X, SHARD, 128)
        later(sum_in.at[q], ss_sem.at[q])
        for n, (xx, cc) in enumerate(sum_peers):
            remote(
                sum_out.at[q, cc, xx], sum_in.at[q, n], ss_sem.at[q], sr_sem.at[q],
                at_snd(xx, zh, cc),
            ).start()

    def across_z(q):
        every = sum_in.at[q]
        remote(every, every, ss_sem.at[q], sr_sem.at[q], opposite).wait_recv()
        own = acc[q, core, pl.ds(pl.multiple_of(x * SHARD, SHARD), SHARD), :]
        own = own + jnp.sum(sum_in[q].astype(F32), axis=0)
        z_own[q] = own
        z_out[q] = own.astype(BF16)
        copy = remote(z_out.at[q], z_in.at[q], hs_sem.at[q], hr_sem.at[q], opposite)
        copy.start()
        drains.append(copy.wait_send)
        return copy

    def share(q, copy):
        copy.wait_recv()
        flux[q, core, x] = (z_own[q] + z_in[q].astype(F32)).astype(BF16)
        shard = flux.at[q, core, x]
        later(sum_in.at[q], gs_sem.at[q])
        for xx, cc in sum_peers:
            remote(shard, shard, gs_sem.at[q], gr_sem.at[q], at_snd(xx, zh, cc)).start()

    def whole_flux(q):
        return jnp.concatenate([flux[q, c].reshape(COLS, 128) for c in range(2)], axis=1)

    def products(q):
        every = sum_in.at[q]
        remote(every, every, gs_sem.at[q], gr_sem.at[q], opposite).wait_recv()
        both = dot_nn(g2[...], whole_flux(q)) * weights[q]
        return both[:, :128] + both[:, 128:]

    for q in range(CHUNKS):
        partial_flux(q)
    pl.semaphore_wait(token, 1)
    moved = [across_z(q) for q in range(CHUNKS)]
    for q in range(CHUNKS):
        share(q, moved[q])

    pair_x[...] = products(0)
    total = pair_x[...] + products(1)
    gather = ((iota((256, 1024), 1) >> 2) == iota((256, 1024), 0)).astype(BF16)
    total_hi = total.astype(BF16)
    total_lo = (total - total_hi.astype(F32)).astype(BF16)
    pair = dot_nn(gather, total_hi) + dot_nn(gather, total_lo)
    pair_out[...] = pair.reshape(CELLS, 8, 128)

    later(pair_in, ps_sem)
    for m in FAR_FIRST + (0,):
        for d in (2, 1, 3, 0):
            if m or d:
                target = ((y + d) % Y) * ZL + (z_peer[m] if m else zl)
                remote(
                    pair_out.at[target], pair_in.at[m * Y + d - 1], ps_sem, pr_sem, (target, snd)
                ).start()

    hq = jnp.zeros((416, COLS), F32)
    for q in range(CHUNKS):
        columns = whole_flux(q)
        hq = hq + dot_nt(spread[0, q], columns) + dot_nt(spread[1, q], columns)
    hq_ref[...] = hq.astype(BF16)

    remote(pair_in, pair_in, ps_sem, pr_sem, opposite).wait_recv()
    pc_ref[...] = pair_out[cell] + jnp.sum(pair_in[...], axis=0)

    finish()


def shards(
    footprint, spatial_cov, week_scale, band_width, sounding_weeks, target_print, target_weeks,
):
    hbm = pl.BlockSpec(memory_space=pltpu.HBM)
    vmem = pl.BlockSpec(memory_space=pltpu.VMEM)
    dma = pltpu.SemaphoreType.DMA
    hq, pair = pl.pallas_call(
        kernel,
        out_shape=(
            jax.ShapeDtypeStruct((416, COLS), BF16),
            jax.ShapeDtypeStruct((8, 128), F32),
        ),
        in_specs=[hbm] * 4 + [pl.BlockSpec(memory_space=pltpu.SMEM)] + [hbm] * 2,
        out_specs=(vmem, vmem),
        scratch_shapes=[
            pltpu.VMEM((CELLS, 4 * KC, 128), BF16),
            pltpu.VMEM((768, COLS), BF16),
            pltpu.VMEM((Y, COLS, GROUP), BF16),
            pltpu.VMEM((256, 4, COLS), BF16),
            pltpu.VMEM((1024, COLS), BF16),
            pltpu.VMEM((1, 52), F32),
            pltpu.VMEM((1, 128), I32),
            pltpu.VMEM((1, 256), I32),
            pltpu.VMEM((CHUNKS, 1024, 256), F32),
            pltpu.VMEM((2, CHUNKS, 416, 256), BF16),
            pltpu.VMEM((CHUNKS, 2, COLS, 128), F32),
            pltpu.VMEM((CHUNKS, 2, X, SHARD, 128), BF16),
            pltpu.VMEM((CHUNKS, 2 * X - 1, SHARD, 128), BF16),
            pltpu.VMEM((CHUNKS, SHARD, 128), BF16),
            pltpu.VMEM((CHUNKS, SHARD, 128), BF16),
            pltpu.VMEM((CHUNKS, SHARD, 128), F32),
            pltpu.VMEM((CHUNKS, 2, X, SHARD, 128), BF16),
            pltpu.VMEM((1024, 128), F32),
            pltpu.VMEM((CELLS, 8, 128), F32),
            pltpu.VMEM((CELLS - 1, 8, 128), F32),
            dma((6,)),
            dma, dma((CHUNKS, ZL - 1)),
            dma, dma((CHUNKS, Y - 1)),
            dma((CHUNKS,)), dma((CHUNKS,)),
            dma((CHUNKS,)), dma((CHUNKS,)),
            dma((CHUNKS,)), dma((CHUNKS,)),
            dma, dma,
            pltpu.SemaphoreType.REGULAR,
        ],
        compiler_params=pltpu.CompilerParams(
            collective_id=0, has_side_effects=True, vmem_limit_bytes=48 << 20
        ),
        name="prior_products",
    )(
        in_hbm(jnp.transpose(footprint, (1, 2, 0)).reshape(4 * KC, 128)),
        in_hbm(spatial_cov),
        in_hbm(target_print),
        in_hbm(week_scale.reshape(1, 52)),
        band_width,
        in_hbm(sounding_weeks.reshape(1, 128)),
        in_hbm(target_weeks.reshape(1, 256)),
    )
    return jnp.transpose(hq.reshape(52, 8, COLS), (1, 0, 2)), pair.T


def solution(mesh):
    placed = (
        P(None, None, ("snd", "cells")),
        P("snd", "cells"),
        P(),
        P(),
        P(),
        P("snd", None, "cells"),
        P("snd"),
    )
    return jax.shard_map(
        shards,
        mesh=mesh,
        in_specs=placed,
        out_specs=(P("snd", None, "cells"), P(None, ("snd", "cells"))),
        check_vma=False,
    )
```

```python
import jax
import jax.numpy as jnp
from jax import lax
from jax.experimental import pallas as pl
from jax.experimental.pallas import tpu as pltpu
from jax.sharding import PartitionSpec as P

MESH = pl.DeviceIdType.MESH
F32, BF16, I32 = jnp.float32, jnp.bfloat16, jnp.int32
X, Y, ZL = 4, 4, 8
CELLS = 32
KC = 24
COLS = 384
SHARD = COLS // X
CHUNKS = 2
ROWS = 2 * KC
GROUP = ZL * KC
AWAY = (1, 3, 2)
BACK = (1, 0, 2)
FAR_FIRST = (7, 6, 5, 4, 3, 2, 1)
HALF_LINE = (4, 3, 2, 1)


def iota(shape, dim):
    return lax.broadcasted_iota(I32, shape, dim)


def dot_nt(a, b, precision=None):
    return lax.dot_general(
        a, b, (((1,), (1,)), ((), ())), precision=precision, preferred_element_type=F32
    )


def dot_nn(a, b, precision=None):
    return lax.dot_general(
        a, b, (((1,), (0,)), ((), ())), precision=precision, preferred_element_type=F32
    )


def flip_bits(pos, mask):
    out = 0
    for bit in (0, 1, 2):
        value = (pos // (1 << bit)) % 2
        out = out + (1 << bit) * (1 - value if mask & (1 << bit) else value)
    return out


def in_hbm(array):
    return pltpu.with_memory_space_constraint(array, pltpu.HBM)


def kernel(
    f_hbm, c_hbm, g_hbm, scale_hbm, band_ref, sw_hbm, tw_hbm,
    hq_ref, pc_ref,
    raw, c_buf, ct, g3, g2, scale_v, sw_v, tw_v,
    weights, spread, acc, sum_out, sum_in, z_out, z_in, z_own,
    flux, pair_x, pair_out, pair_in,
    load_sem, zs_sem, zr_sem, ys_sem, yr_sem, ss_sem, sr_sem,
    hs_sem, hr_sem, gs_sem, gr_sem, ps_sem, pr_sem, token,
):
    cell = lax.axis_index("cells")
    snd = lax.axis_index("snd")
    x, zh, core = snd // 4, (snd // 2) % 2, snd % 2
    y, zl = cell // ZL, cell % ZL

    def at_cells(yy, zz):
        return (yy * ZL + zz, snd)

    def at_snd(xx, hh, cc):
        return (cell, (xx * 2 + hh) * 2 + cc)

    def remote(src, dst, send, recv, device):
        return pltpu.make_async_remote_copy(
            src_ref=src, dst_ref=dst, send_sem=send, recv_sem=recv,
            device_id=device, device_id_type=MESH,
        )

    drains = []

    def finish():
        for drain in drains:
            drain()

    def later(ref, sem):
        drains.append(remote(ref, ref, sem, load_sem.at[0], opposite).wait_send)

    z_peer = {m: flip_bits(zl, m) for m in FAR_FIRST}
    y_peers = [(y + d) % Y for d in AWAY]
    sum_peers = [
        ((x + d) % X, (core + f) % 2) for d in (2, 1, 3, 0) for f in (0, 1) if d or f
    ]
    opposite = at_snd(x, 1 - zh, core)
    across = (y * ZL + z_peer[4], (x * 2 + 1 - zh) * 2 + core)

    barrier = pltpu.get_barrier_semaphore()
    greeted = [at_cells(y, z_peer[m]) for m in HALF_LINE] + [across]
    greeted += [at_cells(p, zl) for p in y_peers]
    greeted += [at_snd(xx, zh, cc) for xx, cc in sum_peers]
    for device in greeted:
        pl.semaphore_signal(barrier, inc=1, device_id=device, device_id_type=MESH)

    load_f = pltpu.make_async_copy(f_hbm, raw.at[cell], load_sem.at[0])
    load_f.start()
    loads = [
        pltpu.make_async_copy(src, dst, load_sem.at[1 + n])
        for n, (src, dst) in enumerate(
            ((scale_hbm, scale_v), (sw_hbm, sw_v), (tw_hbm, tw_v), (c_hbm, c_buf), (g_hbm, g3))
        )
    ]
    for copy in loads:
        copy.start()

    for copy in loads[:3]:
        copy.wait()
    top = lax.Precision.HIGHEST
    scale8 = jnp.broadcast_to(scale_v[...], (8, 52))
    eye = (iota((64, 52), 0) == iota((64, 52), 1)).astype(F32)
    scale_row = dot_nt(scale8, eye, top)
    scale_col = dot_nt(eye, scale8, top)
    lag = jnp.abs(iota((64, 64), 0) - iota((64, 64), 1))
    decay = jnp.exp(lag.astype(F32) * (-1.0 / 6.0))
    table = jnp.where(lag <= band_ref[0], decay, 0.0)
    table = table * scale_col[:, 0:1] * scale_row[0:1, :]
    first = sw_v[...]
    weeks = jnp.concatenate([first + a for a in range(4)], axis=1)
    source_pick = (iota((64, 512), 0) == weeks).astype(F32)
    source_rows = dot_nn(table, source_pick, top)
    row_hi = source_rows.astype(BF16)
    rest = source_rows - row_hi.astype(F32)
    row_mid = rest.astype(BF16)
    row_lo = (rest - row_mid.astype(F32)).astype(BF16)
    rows3 = jnp.concatenate([row_hi, row_mid, row_lo], axis=0)
    repeat = ((iota((1024, 256), 0) >> 2) == iota((1024, 256), 1)).astype(BF16)
    target_first = jnp.broadcast_to(tw_v[...], (8, 256)).astype(F32).astype(BF16)
    target_col = dot_nt(repeat, target_first)[:, 0:1].astype(I32)
    target_week = target_col + (iota((1024, 1), 0) & 3)
    target_pick = ((iota((1024, 192), 1) & 63) == target_week).astype(F32).astype(BF16)
    for q in range(CHUNKS):
        weights[q] = dot_nn(target_pick, rows3[:, q * 256 : (q + 1) * 256])
    loads[3].wait()
    for g in range(Y):
        ct[g] = c_buf[g * GROUP : (g + 1) * GROUP, :].astype(F32).T.astype(BF16)

    load_f.wait()
    pl.semaphore_wait(barrier, len(greeted))
    pl.semaphore_signal(token, inc=1, device_id=across, device_id_type=MESH)

    later(raw.at[pl.ds(0, ZL - 1)], zs_sem)
    later(raw.at[pl.ds(0, ZL * (Y - 1))], ys_sem)

    def piece(q, block):
        return raw.at[block, pl.ds(q * ROWS, ROWS)]

    def along_y(q, block):
        part = piece(q, block)
        for n, peer in enumerate(y_peers):
            remote(part, part, ys_sem, yr_sem.at[q, BACK[n]], at_cells(peer, zl)).start()

    def along_z(q, block, m, slot):
        part = piece(q, block)
        remote(
            part, part, zs_sem, zr_sem.at[q, slot - 1], at_cells(y, z_peer[m])
        ).start()

    def from_z(q, m):
        block = y * ZL + z_peer[m]
        part = piece(q, block)
        remote(part, part, zs_sem, zr_sem.at[q, m - 1], opposite).wait_recv()
        return block

    for q in range(CHUNKS):
        along_z(q, cell, 4, 4)
    for q in range(CHUNKS):
        for m in (1, 2, 3):
            along_z(q, cell, m, m)
        along_y(q, cell)
    for q in range(CHUNKS):
        for m in (1, 4, 2, 3):
            block = from_z(q, m)
            if m == 4:
                for near in (1, 2, 3):
                    along_z(q, block, near, near + 4)
            along_y(q, block)
    for q in range(CHUNKS):
        for m in (5, 6, 7):
            along_y(q, from_z(q, m))

    loads[4].wait()
    g2[...] = g3[...].reshape(1024, COLS)
    mine = (iota((8, 512), 1) & 127) == iota((8, 512), 0) + snd * 8
    mine = mine.astype(F32)
    wide = (source_rows[:52].reshape(52, 1, 512) * mine.reshape(1, 8, 512)).reshape(416, 512)
    wide_hi = wide.astype(BF16)
    wide_lo = (wide - wide_hi.astype(F32)).astype(BF16)
    for q in range(CHUNKS):
        spread[0, q] = wide_hi[:, q * 256 : (q + 1) * 256]
        spread[1, q] = wide_lo[:, q * 256 : (q + 1) * 256]

    def unpack(q, group):
        blocks = raw[pl.ds(group * ZL, ZL), q * ROWS : (q + 1) * ROWS].astype(F32)
        return jnp.concatenate(
            [
                blocks[:, a * KC : (a + 1) * KC, :].reshape(GROUP, 128).astype(BF16)
                for a in range(2)
            ],
            axis=1,
        )

    def partial_flux(q):
        total = dot_nn(ct[y], unpack(q, y))
        for n, peer in enumerate(y_peers):
            part = raw.at[pl.ds(peer * ZL, ZL), pl.ds(q * ROWS, ROWS)]
            remote(part, part, ys_sem, yr_sem.at[q, n], opposite).wait_recv()
            total = total + dot_nn(ct[peer], unpack(q, peer))
        for c in range(2):
            half = total[:, c * 128 : (c + 1) * 128]
            acc[q, c] = half
            sum_out[q, c] = half.astype(BF16).reshape(X, SHARD, 128)
        later(sum_in.at[q], ss_sem.at[q])
        for n, (xx, cc) in enumerate(sum_peers):
            remote(
                sum_out.at[q, cc, xx], sum_in.at[q, n], ss_sem.at[q], sr_sem.at[q],
                at_snd(xx, zh, cc),
            ).start()

    def across_z(q):
        every = sum_in.at[q]
        remote(every, every, ss_sem.at[q], sr_sem.at[q], opposite).wait_recv()
        own = acc[q, core, pl.ds(pl.multiple_of(x * SHARD, SHARD), SHARD), :]
        own = own + jnp.sum(sum_in[q].astype(F32), axis=0)
        z_own[q] = own
        z_out[q] = own.astype(BF16)
        copy = remote(z_out.at[q], z_in.at[q], hs_sem.at[q], hr_sem.at[q], opposite)
        copy.start()
        drains.append(copy.wait_send)
        return copy

    def share(q, copy):
        copy.wait_recv()
        flux[q, core, x] = (z_own[q] + z_in[q].astype(F32)).astype(BF16)
        shard = flux.at[q, core, x]
        later(sum_in.at[q], gs_sem.at[q])
        for xx, cc in sum_peers:
            remote(shard, shard, gs_sem.at[q], gr_sem.at[q], at_snd(xx, zh, cc)).start()

    def whole_flux(q):
        return jnp.concatenate([flux[q, c].reshape(COLS, 128) for c in range(2)], axis=1)

    def products(q):
        every = sum_in.at[q]
        remote(every, every, gs_sem.at[q], gr_sem.at[q], opposite).wait_recv()
        both = dot_nn(g2[...], whole_flux(q)) * weights[q]
        return both[:, :128] + both[:, 128:]

    for q in range(CHUNKS):
        partial_flux(q)
    pl.semaphore_wait(token, 1)
    moved = [across_z(q) for q in range(CHUNKS)]
    for q in range(CHUNKS):
        share(q, moved[q])

    pair_x[...] = products(0)
    total = pair_x[...] + products(1)
    gather = ((iota((256, 1024), 1) >> 2) == iota((256, 1024), 0)).astype(BF16)
    total_hi = total.astype(BF16)
    total_lo = (total - total_hi.astype(F32)).astype(BF16)
    pair = dot_nn(gather, total_hi) + dot_nn(gather, total_lo)
    pair_out[...] = pair.reshape(CELLS, 8, 128)

    later(pair_in, ps_sem)
    for m in FAR_FIRST + (0,):
        for d in (2, 1, 3, 0):
            if m or d:
                target = ((y + d) % Y) * ZL + (z_peer[m] if m else zl)
                remote(
                    pair_out.at[target], pair_in.at[m * Y + d - 1], ps_sem, pr_sem, (target, snd)
                ).start()

    hq = jnp.zeros((416, COLS), F32)
    for q in range(CHUNKS):
        columns = whole_flux(q)
        hq = hq + dot_nt(spread[0, q], columns) + dot_nt(spread[1, q], columns)
    hq_ref[...] = hq.astype(BF16)

    remote(pair_in, pair_in, ps_sem, pr_sem, opposite).wait_recv()
    pc_ref[...] = pair_out[cell] + jnp.sum(pair_in[...], axis=0)

    finish()


def publish(hq_ref, pair_ref, hq_out, pair_out, sem):
    copies = [
        pltpu.make_async_copy(src, dst, sem.at[n])
        for n, (src, dst) in enumerate(((hq_ref, hq_out), (pair_ref, pair_out)))
    ]
    for copy in copies:
        copy.start()
    for copy in copies:
        copy.wait()


def shards(
    footprint, spatial_cov, week_scale, band_width, sounding_weeks, target_print, target_weeks,
):
    hbm = pl.BlockSpec(memory_space=pltpu.HBM)
    vmem = pl.BlockSpec(memory_space=pltpu.VMEM)
    dma = pltpu.SemaphoreType.DMA
    hq, pair = pl.pallas_call(
        kernel,
        out_shape=(
            jax.ShapeDtypeStruct((416, COLS), BF16),
            jax.ShapeDtypeStruct((8, 128), F32),
        ),
        in_specs=[hbm] * 4 + [pl.BlockSpec(memory_space=pltpu.SMEM)] + [hbm] * 2,
        out_specs=(vmem, vmem),
        scratch_shapes=[
            pltpu.VMEM((CELLS, 4 * KC, 128), BF16),
            pltpu.VMEM((768, COLS), BF16),
            pltpu.VMEM((Y, COLS, GROUP), BF16),
            pltpu.VMEM((256, 4, COLS), BF16),
            pltpu.VMEM((1024, COLS), BF16),
            pltpu.VMEM((1, 52), F32),
            pltpu.VMEM((1, 128), I32),
            pltpu.VMEM((1, 256), I32),
            pltpu.VMEM((CHUNKS, 1024, 256), F32),
            pltpu.VMEM((2, CHUNKS, 416, 256), BF16),
            pltpu.VMEM((CHUNKS, 2, COLS, 128), F32),
            pltpu.VMEM((CHUNKS, 2, X, SHARD, 128), BF16),
            pltpu.VMEM((CHUNKS, 2 * X - 1, SHARD, 128), BF16),
            pltpu.VMEM((CHUNKS, SHARD, 128), BF16),
            pltpu.VMEM((CHUNKS, SHARD, 128), BF16),
            pltpu.VMEM((CHUNKS, SHARD, 128), F32),
            pltpu.VMEM((CHUNKS, 2, X, SHARD, 128), BF16),
            pltpu.VMEM((1024, 128), F32),
            pltpu.VMEM((CELLS, 8, 128), F32),
            pltpu.VMEM((CELLS - 1, 8, 128), F32),
            dma((6,)),
            dma, dma((CHUNKS, ZL - 1)),
            dma, dma((CHUNKS, Y - 1)),
            dma((CHUNKS,)), dma((CHUNKS,)),
            dma((CHUNKS,)), dma((CHUNKS,)),
            dma((CHUNKS,)), dma((CHUNKS,)),
            dma, dma,
            pltpu.SemaphoreType.REGULAR,
        ],
        compiler_params=pltpu.CompilerParams(
            collective_id=0, has_side_effects=True, vmem_limit_bytes=48 << 20
        ),
        name="prior_products",
    )(
        in_hbm(jnp.transpose(footprint, (1, 2, 0)).reshape(4 * KC, 128)),
        in_hbm(spatial_cov),
        in_hbm(target_print),
        in_hbm(week_scale.reshape(1, 52)),
        band_width,
        in_hbm(sounding_weeks.reshape(1, 128)),
        in_hbm(target_weeks.reshape(1, 256)),
    )
    hq, pair = pl.pallas_call(
        publish,
        out_shape=(
            jax.ShapeDtypeStruct((416, COLS), BF16),
            jax.ShapeDtypeStruct((8, 128), F32),
        ),
        in_specs=[vmem, vmem],
        out_specs=(pl.BlockSpec(memory_space=pl.ANY), pl.BlockSpec(memory_space=pl.ANY)),
        scratch_shapes=[dma((2,))],
        name="publish",
    )(hq, pair)
    return jnp.transpose(hq.reshape(52, 8, COLS), (1, 0, 2)), pair.T


def solution(mesh):
    placed = (
        P(None, None, ("snd", "cells")),
        P("snd", "cells"),
        P(),
        P(),
        P(),
        P("snd", None, "cells"),
        P("snd"),
    )
    return jax.shard_map(
        shards,
        mesh=mesh,
        in_specs=placed,
        out_specs=(P("snd", None, "cells"), P(None, ("snd", "cells"))),
        check_vma=False,
    )
```

```python
import jax
import jax.numpy as jnp
from jax import lax
from jax.experimental import pallas as pl
from jax.experimental.pallas import tpu as pltpu
from jax.sharding import PartitionSpec as P

MESH = pl.DeviceIdType.MESH
F32, BF16, I32 = jnp.float32, jnp.bfloat16, jnp.int32
X, Y, ZL = 4, 4, 8
CELLS = 32
KC = 24
COLS = 384
SHARD = COLS // X
CHUNKS = 2
ROWS = 2 * KC
HALF = SHARD // 2
PIECES = [(q, h) for q in range(CHUNKS) for h in range(2)]
GROUP = ZL * KC
AWAY = (1, 3, 2)
BACK = (1, 0, 2)
FAR_FIRST = (7, 6, 5, 4, 3, 2, 1)
HALF_LINE = (4, 3, 2, 1)


def iota(shape, dim):
    return lax.broadcasted_iota(I32, shape, dim)


def dot_nt(a, b, precision=None):
    return lax.dot_general(
        a, b, (((1,), (1,)), ((), ())), precision=precision, preferred_element_type=F32
    )


def dot_nn(a, b, precision=None):
    return lax.dot_general(
        a, b, (((1,), (0,)), ((), ())), precision=precision, preferred_element_type=F32
    )


def flip_bits(pos, mask):
    out = 0
    for bit in (0, 1, 2):
        value = (pos // (1 << bit)) % 2
        out = out + (1 << bit) * (1 - value if mask & (1 << bit) else value)
    return out


def in_hbm(array):
    return pltpu.with_memory_space_constraint(array, pltpu.HBM)


def kernel(
    f_hbm, c_hbm, g_hbm, scale_hbm, band_ref, sw_hbm, tw_hbm,
    hq_ref, pc_ref,
    raw, c_buf, ct, g3, g2, scale_v, sw_v, tw_v,
    weights, spread, acc, sum_out, sum_in, z_out, z_in, z_own,
    flux, pair_x, pair_out, pair_in,
    load_sem, zs_sem, zr_sem, ys_sem, yr_sem, ss_sem, sr_sem,
    hs_sem, hr_sem, gs_sem, gr_sem, ps_sem, pr_sem, token,
):
    cell = lax.axis_index("cells")
    snd = lax.axis_index("snd")
    x, zh, core = snd // 4, (snd // 2) % 2, snd % 2
    y, zl = cell // ZL, cell % ZL

    def at_cells(yy, zz):
        return (yy * ZL + zz, snd)

    def at_snd(xx, hh, cc):
        return (cell, (xx * 2 + hh) * 2 + cc)

    def remote(src, dst, send, recv, device):
        return pltpu.make_async_remote_copy(
            src_ref=src, dst_ref=dst, send_sem=send, recv_sem=recv,
            device_id=device, device_id_type=MESH,
        )

    drains = []

    def finish():
        for drain in drains:
            drain()

    def later(ref, sem):
        drains.append(remote(ref, ref, sem, load_sem.at[0], opposite).wait_send)

    z_peer = {m: flip_bits(zl, m) for m in FAR_FIRST}
    y_peers = [(y + d) % Y for d in AWAY]
    sum_peers = [
        ((x + d) % X, (core + f) % 2) for d in (2, 1, 3, 0) for f in (0, 1) if d or f
    ]
    opposite = at_snd(x, 1 - zh, core)
    across = (y * ZL + z_peer[4], (x * 2 + 1 - zh) * 2 + core)

    barrier = pltpu.get_barrier_semaphore()
    greeted = [at_cells(y, z_peer[m]) for m in HALF_LINE] + [across]
    greeted += [at_cells(p, zl) for p in y_peers]
    greeted += [at_snd(xx, zh, cc) for xx, cc in sum_peers]
    for device in greeted:
        pl.semaphore_signal(barrier, inc=1, device_id=device, device_id_type=MESH)

    load_f = pltpu.make_async_copy(f_hbm, raw.at[cell], load_sem.at[0])
    load_f.start()
    loads = [
        pltpu.make_async_copy(src, dst, load_sem.at[1 + n])
        for n, (src, dst) in enumerate(
            ((scale_hbm, scale_v), (sw_hbm, sw_v), (tw_hbm, tw_v), (c_hbm, c_buf), (g_hbm, g3))
        )
    ]
    for copy in loads:
        copy.start()

    for copy in loads[:3]:
        copy.wait()
    top = lax.Precision.HIGHEST
    scale8 = jnp.broadcast_to(scale_v[...], (8, 52))
    eye = (iota((64, 52), 0) == iota((64, 52), 1)).astype(F32)
    scale_row = dot_nt(scale8, eye, top)
    scale_col = dot_nt(eye, scale8, top)
    lag = jnp.abs(iota((64, 64), 0) - iota((64, 64), 1))
    decay = jnp.exp(lag.astype(F32) * (-1.0 / 6.0))
    table = jnp.where(lag <= band_ref[0], decay, 0.0)
    table = table * scale_col[:, 0:1] * scale_row[0:1, :]
    first = sw_v[...]
    weeks = jnp.concatenate([first + a for a in range(4)], axis=1)
    source_pick = (iota((64, 512), 0) == weeks).astype(F32)
    source_rows = dot_nn(table, source_pick, top)
    row_hi = source_rows.astype(BF16)
    rest = source_rows - row_hi.astype(F32)
    row_mid = rest.astype(BF16)
    row_lo = (rest - row_mid.astype(F32)).astype(BF16)
    rows3 = jnp.concatenate([row_hi, row_mid, row_lo], axis=0)
    repeat = ((iota((1024, 256), 0) >> 2) == iota((1024, 256), 1)).astype(BF16)
    target_first = jnp.broadcast_to(tw_v[...], (8, 256)).astype(F32).astype(BF16)
    target_col = dot_nt(repeat, target_first)[:, 0:1].astype(I32)
    target_week = target_col + (iota((1024, 1), 0) & 3)
    target_pick = ((iota((1024, 192), 1) & 63) == target_week).astype(F32).astype(BF16)
    for q in range(CHUNKS):
        weights[q] = dot_nn(target_pick, rows3[:, q * 256 : (q + 1) * 256])
    loads[3].wait()
    for g in range(Y):
        ct[g] = c_buf[g * GROUP : (g + 1) * GROUP, :].astype(F32).T.astype(BF16)

    load_f.wait()
    pl.semaphore_wait(barrier, len(greeted))
    pl.semaphore_signal(token, inc=1, device_id=across, device_id_type=MESH)

    later(raw.at[pl.ds(0, ZL - 1)], zs_sem)
    later(raw.at[pl.ds(0, ZL * (Y - 1))], ys_sem)

    def piece(q, block):
        return raw.at[block, pl.ds(q * ROWS, ROWS)]

    def along_y(q, block):
        part = piece(q, block)
        for n, peer in enumerate(y_peers):
            remote(part, part, ys_sem, yr_sem.at[q, BACK[n]], at_cells(peer, zl)).start()

    def along_z(q, block, m, slot):
        part = piece(q, block)
        remote(
            part, part, zs_sem, zr_sem.at[q, slot - 1], at_cells(y, z_peer[m])
        ).start()

    def from_z(q, m):
        block = y * ZL + z_peer[m]
        part = piece(q, block)
        remote(part, part, zs_sem, zr_sem.at[q, m - 1], opposite).wait_recv()
        return block

    for q in range(CHUNKS):
        along_z(q, cell, 4, 4)
    for q in range(CHUNKS):
        for m in (1, 2, 3):
            along_z(q, cell, m, m)
        along_y(q, cell)
    for q in range(CHUNKS):
        for m in (1, 4, 2, 3):
            block = from_z(q, m)
            if m == 4:
                for near in (1, 2, 3):
                    along_z(q, block, near, near + 4)
            along_y(q, block)
    for q in range(CHUNKS):
        for m in (5, 6, 7):
            along_y(q, from_z(q, m))

    loads[4].wait()
    g2[...] = g3[...].reshape(1024, COLS)
    mine = (iota((8, 512), 1) & 127) == iota((8, 512), 0) + snd * 8
    mine = mine.astype(F32)
    wide = (source_rows[:52].reshape(52, 1, 512) * mine.reshape(1, 8, 512)).reshape(416, 512)
    wide_hi = wide.astype(BF16)
    wide_lo = (wide - wide_hi.astype(F32)).astype(BF16)
    for q in range(CHUNKS):
        spread[0, q] = wide_hi[:, q * 256 : (q + 1) * 256]
        spread[1, q] = wide_lo[:, q * 256 : (q + 1) * 256]

    def unpack(q, group):
        blocks = raw[pl.ds(group * ZL, ZL), q * ROWS : (q + 1) * ROWS].astype(F32)
        return jnp.concatenate(
            [
                blocks[:, a * KC : (a + 1) * KC, :].reshape(GROUP, 128).astype(BF16)
                for a in range(2)
            ],
            axis=1,
        )

    def partial_flux(q):
        total = dot_nn(ct[y], unpack(q, y))
        for n, peer in enumerate(y_peers):
            part = raw.at[pl.ds(peer * ZL, ZL), pl.ds(q * ROWS, ROWS)]
            remote(part, part, ys_sem, yr_sem.at[q, n], opposite).wait_recv()
            total = total + dot_nn(ct[peer], unpack(q, peer))
        for c in range(2):
            half = total[:, c * 128 : (c + 1) * 128]
            acc[q, c] = half
            sum_out[q, c] = half.astype(BF16).reshape(X, SHARD, 128)
        for h in range(2):
            p = 2 * q + h
            later(sum_in.at[p], ss_sem.at[p])
            for n, (xx, cc) in enumerate(sum_peers):
                remote(
                    sum_out.at[q, cc, xx, pl.ds(h * HALF, HALF)], sum_in.at[p, n],
                    ss_sem.at[p], sr_sem.at[p], at_snd(xx, zh, cc),
                ).start()

    def across_z(q, h):
        p = 2 * q + h
        every = sum_in.at[p]
        remote(every, every, ss_sem.at[p], sr_sem.at[p], opposite).wait_recv()
        rows = pl.ds(pl.multiple_of(x * SHARD + h * HALF, HALF), HALF)
        own = acc[q, core, rows, :] + jnp.sum(sum_in[p].astype(F32), axis=0)
        z_own[p] = own
        z_out[p] = own.astype(BF16)
        copy = remote(z_out.at[p], z_in.at[p], hs_sem.at[p], hr_sem.at[p], opposite)
        copy.start()
        drains.append(copy.wait_send)
        return copy

    def share(q, h, copy):
        p = 2 * q + h
        copy.wait_recv()
        flux[q, core, x, h * HALF : (h + 1) * HALF] = (z_own[p] + z_in[p].astype(F32)).astype(BF16)
        part = flux.at[q, core, x, pl.ds(h * HALF, HALF)]
        later(sum_in.at[p], gs_sem.at[p])
        for xx, cc in sum_peers:
            remote(part, part, gs_sem.at[p], gr_sem.at[p], at_snd(xx, zh, cc)).start()

    def whole_flux(q):
        return jnp.concatenate([flux[q, c].reshape(COLS, 128) for c in range(2)], axis=1)

    def products(q):
        for h in range(2):
            p = 2 * q + h
            every = sum_in.at[p]
            remote(every, every, gs_sem.at[p], gr_sem.at[p], opposite).wait_recv()
        both = dot_nn(g2[...], whole_flux(q)) * weights[q]
        return both[:, :128] + both[:, 128:]

    for q in range(CHUNKS):
        partial_flux(q)
    pl.semaphore_wait(token, 1)
    moved = [across_z(q, h) for q, h in PIECES]
    for q, h in PIECES:
        share(q, h, moved[2 * q + h])
    pair_x[...] = products(0)
    total = pair_x[...] + products(1)
    gather = ((iota((256, 1024), 1) >> 2) == iota((256, 1024), 0)).astype(BF16)
    total_hi = total.astype(BF16)
    total_lo = (total - total_hi.astype(F32)).astype(BF16)
    pair = dot_nn(gather, total_hi) + dot_nn(gather, total_lo)
    pair_out[...] = pair.reshape(CELLS, 8, 128)

    later(pair_in, ps_sem)
    for m in FAR_FIRST + (0,):
        for d in (2, 1, 3, 0):
            if m or d:
                target = ((y + d) % Y) * ZL + (z_peer[m] if m else zl)
                remote(
                    pair_out.at[target], pair_in.at[m * Y + d - 1], ps_sem, pr_sem, (target, snd)
                ).start()

    hq = jnp.zeros((416, COLS), F32)
    for q in range(CHUNKS):
        columns = whole_flux(q)
        hq = hq + dot_nt(spread[0, q], columns) + dot_nt(spread[1, q], columns)
    hq_ref[...] = hq.astype(BF16)

    remote(pair_in, pair_in, ps_sem, pr_sem, opposite).wait_recv()
    pc_ref[...] = pair_out[cell] + jnp.sum(pair_in[...], axis=0)

    finish()


def shards(
    footprint, spatial_cov, week_scale, band_width, sounding_weeks, target_print, target_weeks,
):
    hbm = pl.BlockSpec(memory_space=pltpu.HBM)
    vmem = pl.BlockSpec(memory_space=pltpu.VMEM)
    dma = pltpu.SemaphoreType.DMA
    hq, pair = pl.pallas_call(
        kernel,
        out_shape=(
            jax.ShapeDtypeStruct((416, COLS), BF16),
            jax.ShapeDtypeStruct((8, 128), F32),
        ),
        in_specs=[hbm] * 4 + [pl.BlockSpec(memory_space=pltpu.SMEM)] + [hbm] * 2,
        out_specs=(vmem, vmem),
        scratch_shapes=[
            pltpu.VMEM((CELLS, 4 * KC, 128), BF16),
            pltpu.VMEM((768, COLS), BF16),
            pltpu.VMEM((Y, COLS, GROUP), BF16),
            pltpu.VMEM((256, 4, COLS), BF16),
            pltpu.VMEM((1024, COLS), BF16),
            pltpu.VMEM((1, 52), F32),
            pltpu.VMEM((1, 128), I32),
            pltpu.VMEM((1, 256), I32),
            pltpu.VMEM((CHUNKS, 1024, 256), F32),
            pltpu.VMEM((2, CHUNKS, 416, 256), BF16),
            pltpu.VMEM((CHUNKS, 2, COLS, 128), F32),
            pltpu.VMEM((CHUNKS, 2, X, SHARD, 128), BF16),
            pltpu.VMEM((len(PIECES), 2 * X - 1, HALF, 128), BF16),
            pltpu.VMEM((len(PIECES), HALF, 128), BF16),
            pltpu.VMEM((len(PIECES), HALF, 128), BF16),
            pltpu.VMEM((len(PIECES), HALF, 128), F32),
            pltpu.VMEM((CHUNKS, 2, X, SHARD, 128), BF16),
            pltpu.VMEM((1024, 128), F32),
            pltpu.VMEM((CELLS, 8, 128), F32),
            pltpu.VMEM((CELLS - 1, 8, 128), F32),
            dma((6,)),
            dma, dma((CHUNKS, ZL - 1)),
            dma, dma((CHUNKS, Y - 1)),
            dma((len(PIECES),)), dma((len(PIECES),)),
            dma((len(PIECES),)), dma((len(PIECES),)),
            dma((len(PIECES),)), dma((len(PIECES),)),
            dma, dma,
            pltpu.SemaphoreType.REGULAR,
        ],
        compiler_params=pltpu.CompilerParams(
            collective_id=0, has_side_effects=True, vmem_limit_bytes=48 << 20
        ),
        name="prior_products",
    )(
        in_hbm(jnp.transpose(footprint, (1, 2, 0)).reshape(4 * KC, 128)),
        in_hbm(spatial_cov),
        in_hbm(target_print),
        in_hbm(week_scale.reshape(1, 52)),
        band_width,
        in_hbm(sounding_weeks.reshape(1, 128)),
        in_hbm(target_weeks.reshape(1, 256)),
    )
    return jnp.transpose(hq.reshape(52, 8, COLS), (1, 0, 2)), pair.T


def solution(mesh):
    placed = (
        P(None, None, ("snd", "cells")),
        P("snd", "cells"),
        P(),
        P(),
        P(),
        P("snd", None, "cells"),
        P("snd"),
    )
    return jax.shard_map(
        shards,
        mesh=mesh,
        in_specs=placed,
        out_specs=(P("snd", None, "cells"), P(None, ("snd", "cells"))),
        check_vma=False,
    )
```

```python
import jax
import jax.numpy as jnp
from jax import lax
from jax.experimental import pallas as pl
from jax.experimental.pallas import tpu as pltpu
from jax.sharding import PartitionSpec as P

MESH = pl.DeviceIdType.MESH
F32, BF16, I32 = jnp.float32, jnp.bfloat16, jnp.int32
X, Y, ZL = 4, 4, 8
CELLS = 32
KC = 24
COLS = 384
SHARD = COLS // X
CHUNKS = 2
ROWS = 2 * KC
HALF = SHARD // 2
PIECES = [(q, h) for q in range(CHUNKS) for h in range(2)]
QUAD = ZL // 2
GROUP = Y * QUAD * KC
TARGETS = 256
AWAY = (1, 3, 2)
FAR_FIRST = (7, 6, 5, 4, 3, 2, 1)
HALF_LINE = (4, 3, 2, 1)


def iota(shape, dim):
    return lax.broadcasted_iota(I32, shape, dim)


def dot_nt(a, b, precision=None):
    return lax.dot_general(
        a, b, (((1,), (1,)), ((), ())), precision=precision, preferred_element_type=F32
    )


def dot_nn(a, b, precision=None):
    return lax.dot_general(
        a, b, (((1,), (0,)), ((), ())), precision=precision, preferred_element_type=F32
    )


def flip_bits(pos, mask):
    out = 0
    for bit in (0, 1, 2):
        value = (pos // (1 << bit)) % 2
        out = out + (1 << bit) * (1 - value if mask & (1 << bit) else value)
    return out


def in_hbm(array):
    return pltpu.with_memory_space_constraint(array, pltpu.HBM)


def kernel(
    f_hbm, c_hbm, g_hbm, scale_hbm, band_ref, sw_hbm, tw_hbm,
    hq_ref, pc_ref,
    raw, c_buf, ct, g3, g2, scale_v, sw_v, tw_v,
    weights, spread, acc, sum_out, sum_in, z_out, z_in, z_own,
    flux, pair_x, pair_out, pair_in,
    load_sem, zs_sem, zr_sem, ys_sem, yr_sem, ss_sem, sr_sem,
    hs_sem, hr_sem, gs_sem, gr_sem, ps_sem, pr_sem, token,
):
    cell = lax.axis_index("cells")
    snd = lax.axis_index("snd")
    x, zh, core = snd // 4, (snd // 2) % 2, snd % 2
    y, zl = cell // ZL, cell % ZL

    def at_cells(yy, zz):
        return (yy * ZL + zz, snd)

    def at_snd(xx, hh, cc):
        return (cell, (xx * 2 + hh) * 2 + cc)

    def remote(src, dst, send, recv, device):
        return pltpu.make_async_remote_copy(
            src_ref=src, dst_ref=dst, send_sem=send, recv_sem=recv,
            device_id=device, device_id_type=MESH,
        )

    drains = []

    def finish():
        for drain in drains:
            drain()

    def later(ref, sem):
        drains.append(remote(ref, ref, sem, load_sem.at[0], opposite).wait_send)

    z_peer = {m: flip_bits(zl, m) for m in FAR_FIRST}
    y_peers = [(y + d) % Y for d in AWAY]
    sum_peers = [
        ((x + d) % X, (core + f) % 2) for d in (2, 1, 3, 0) for f in (0, 1) if d or f
    ]
    opposite = at_snd(x, 1 - zh, core)
    across = (y * ZL + z_peer[4], (x * 2 + 1 - zh) * 2 + core)

    barrier = pltpu.get_barrier_semaphore()
    greeted = [at_cells(y, z_peer[m]) for m in HALF_LINE] + [across]
    greeted += [at_cells(p, zl) for p in y_peers]
    greeted += [at_snd(xx, zh, cc) for xx, cc in sum_peers]
    for device in greeted:
        pl.semaphore_signal(barrier, inc=1, device_id=device, device_id_type=MESH)

    load_f = pltpu.make_async_copy(f_hbm, raw.at[cell], load_sem.at[0])
    load_f.start()
    loads = [
        pltpu.make_async_copy(src, dst, load_sem.at[1 + n])
        for n, (src, dst) in enumerate(
            ((scale_hbm, scale_v), (sw_hbm, sw_v), (tw_hbm, tw_v), (c_hbm, c_buf), (g_hbm, g3))
        )
    ]
    for copy in loads:
        copy.start()

    for copy in loads[:3]:
        copy.wait()
    top = lax.Precision.HIGHEST
    scale8 = jnp.broadcast_to(scale_v[...], (8, 52))
    eye = (iota((64, 52), 0) == iota((64, 52), 1)).astype(F32)
    scale_row = dot_nt(scale8, eye, top)
    scale_col = dot_nt(eye, scale8, top)
    lag = jnp.abs(iota((64, 64), 0) - iota((64, 64), 1))
    decay = jnp.exp(lag.astype(F32) * (-1.0 / 6.0))
    table = jnp.where(lag <= band_ref[0], decay, 0.0)
    table = table * scale_col[:, 0:1] * scale_row[0:1, :]
    first = sw_v[...]
    weeks = jnp.concatenate([first + a for a in range(4)], axis=1)
    source_pick = (iota((64, 512), 0) == weeks).astype(F32)
    source_rows = dot_nn(table, source_pick, top)
    row_hi = source_rows.astype(BF16)
    rest = source_rows - row_hi.astype(F32)
    row_mid = rest.astype(BF16)
    row_lo = (rest - row_mid.astype(F32)).astype(BF16)
    rows3 = jnp.concatenate([row_hi, row_mid, row_lo], axis=0)
    repeat = ((iota((1024, 256), 0) & 255) == iota((1024, 256), 1)).astype(BF16)
    target_first = jnp.broadcast_to(tw_v[...], (8, 256)).astype(F32).astype(BF16)
    target_col = dot_nt(repeat, target_first)[:, 0:1].astype(I32)
    target_week = target_col + (iota((1024, 1), 0) >> 8)
    target_pick = ((iota((1024, 192), 1) & 63) == target_week).astype(F32).astype(BF16)
    for q in range(CHUNKS):
        weights[q] = dot_nn(target_pick, rows3[:, q * 256 : (q + 1) * 256])
    loads[3].wait()
    for quad in range(2):
        rows = [
            c_buf[(g * 2 + quad) * QUAD * KC : (g * 2 + quad + 1) * QUAD * KC, :].astype(F32)
            for g in range(Y)
        ]
        ct[quad] = jnp.concatenate(rows, axis=0).T.astype(BF16)

    load_f.wait()
    pl.semaphore_wait(barrier, len(greeted))
    pl.semaphore_signal(token, inc=1, device_id=across, device_id_type=MESH)

    later(raw.at[pl.ds(0, ZL - 1)], zs_sem)
    later(raw.at[pl.ds(0, ZL * (Y - 1))], ys_sem)

    def piece(q, block):
        return raw.at[block, pl.ds(q * ROWS, ROWS)]

    def along_y(q, block, far):
        part = piece(q, block)
        for peer in y_peers:
            remote(part, part, ys_sem, yr_sem.at[q, far], at_cells(peer, zl)).start()

    def along_z(q, block, m, slot):
        part = piece(q, block)
        remote(
            part, part, zs_sem, zr_sem.at[q, slot - 1], at_cells(y, z_peer[m])
        ).start()

    def from_z(q, m):
        block = y * ZL + z_peer[m]
        part = piece(q, block)
        remote(part, part, zs_sem, zr_sem.at[q, m - 1], opposite).wait_recv()
        return block

    for q in range(CHUNKS):
        along_z(q, cell, 4, 4)
    for q in range(CHUNKS):
        for m in (1, 2, 3):
            along_z(q, cell, m, m)
        along_y(q, cell, 0)

    loads[4].wait()
    targets = g3[...].reshape(4 * TARGETS, COLS)
    offset = iota((TARGETS, 4 * TARGETS), 1) - 4 * iota((TARGETS, 4 * TARGETS), 0)
    for k in range(4):
        g2[k * TARGETS : (k + 1) * TARGETS] = dot_nn(
            (offset == k).astype(F32).astype(BF16), targets
        ).astype(BF16)

    for q in range(CHUNKS):
        for m in (1, 4, 2, 3):
            block = from_z(q, m)
            if m == 4:
                for near in (1, 2, 3):
                    along_z(q, block, near, near + 4)
            along_y(q, block, m // 4)
    for q in range(CHUNKS):
        for m in (5, 6, 7):
            along_y(q, from_z(q, m), 1)

    mine = (iota((8, 512), 1) & 127) == iota((8, 512), 0) + snd * 8
    mine = mine.astype(F32)
    wide = (source_rows[:52].reshape(52, 1, 512) * mine.reshape(1, 8, 512)).reshape(416, 512)
    wide_hi = wide.astype(BF16)
    wide_lo = (wide - wide_hi.astype(F32)).astype(BF16)
    for q in range(CHUNKS):
        spread[0, q] = wide_hi[:, q * 256 : (q + 1) * 256]
        spread[1, q] = wide_lo[:, q * 256 : (q + 1) * 256]

    def unpack(q, quad):
        blocks = [
            raw[pl.ds((g * 2 + quad) * QUAD, QUAD), q * ROWS : (q + 1) * ROWS].astype(F32)
            for g in range(Y)
        ]
        halves = [
            jnp.concatenate(
                [b[:, a * KC : (a + 1) * KC, :].reshape(QUAD * KC, 128) for b in blocks], axis=0
            ).astype(BF16)
            for a in range(2)
        ]
        return jnp.concatenate(halves, axis=1)

    own_quad = zl // QUAD

    def from_y(q, far):
        part = raw.at[pl.ds(0, QUAD * (Y - 1)), pl.ds(0, ROWS)]
        remote(part, part, ys_sem, yr_sem.at[q, far], opposite).wait_recv()

    def near_flux(q):
        from_y(q, 0)
        total = dot_nn(ct[own_quad], unpack(q, own_quad))
        for c in range(2):
            acc[q, c] = total[:, c * 128 : (c + 1) * 128]

    def partial_flux(q):
        from_y(q, 1)
        total = jnp.concatenate([acc[q, 0], acc[q, 1]], axis=1)
        total = total + dot_nn(ct[1 - own_quad], unpack(q, 1 - own_quad))
        for c in range(2):
            half = total[:, c * 128 : (c + 1) * 128]
            acc[q, c] = half
            sum_out[q, c] = half.astype(BF16).reshape(X, SHARD, 128)
        for h in range(2):
            p = 2 * q + h
            later(sum_in.at[p], ss_sem.at[p])
            for n, (xx, cc) in enumerate(sum_peers):
                remote(
                    sum_out.at[q, cc, xx, pl.ds(h * HALF, HALF)], sum_in.at[p, n],
                    ss_sem.at[p], sr_sem.at[p], at_snd(xx, zh, cc),
                ).start()

    def across_z(q, h):
        p = 2 * q + h
        every = sum_in.at[p]
        remote(every, every, ss_sem.at[p], sr_sem.at[p], opposite).wait_recv()
        rows = pl.ds(pl.multiple_of(x * SHARD + h * HALF, HALF), HALF)
        own = acc[q, core, rows, :] + jnp.sum(sum_in[p].astype(F32), axis=0)
        z_own[p] = own
        z_out[p] = own.astype(BF16)
        copy = remote(z_out.at[p], z_in.at[p], hs_sem.at[p], hr_sem.at[p], opposite)
        copy.start()
        drains.append(copy.wait_send)
        return copy

    def share(q, h, copy):
        p = 2 * q + h
        copy.wait_recv()
        flux[q, core, x, h * HALF : (h + 1) * HALF] = (z_own[p] + z_in[p].astype(F32)).astype(BF16)
        part = flux.at[q, core, x, pl.ds(h * HALF, HALF)]
        later(sum_in.at[p], gs_sem.at[p])
        for xx, cc in sum_peers:
            remote(part, part, gs_sem.at[p], gr_sem.at[p], at_snd(xx, zh, cc)).start()

    def whole_flux(q):
        return jnp.concatenate([flux[q, c].reshape(COLS, 128) for c in range(2)], axis=1)

    def products(q):
        for h in range(2):
            p = 2 * q + h
            every = sum_in.at[p]
            remote(every, every, gs_sem.at[p], gr_sem.at[p], opposite).wait_recv()
        both = dot_nn(g2[...], whole_flux(q)) * weights[q]
        both = both[:, :128] + both[:, 128:]
        return jnp.sum(both.reshape(4, TARGETS, 128), axis=0)

    for q in range(CHUNKS):
        near_flux(q)
    for q in range(CHUNKS):
        partial_flux(q)
    pl.semaphore_wait(token, 1)
    moved = [across_z(q, h) for q, h in PIECES]
    for q, h in PIECES:
        share(q, h, moved[2 * q + h])
    pair_x[...] = products(0)
    total = (pair_x[...] + products(1)).reshape(CELLS, 8, 128)
    pair_x[...] = total.reshape(TARGETS, 128)
    pair_out[...] = total.astype(BF16)

    later(pair_in, ps_sem)
    for d in (2, 1, 3, 0):
        for m in FAR_FIRST + (0,):
            if m or d:
                target = ((y + d) % Y) * ZL + (z_peer[m] if m else zl)
                remote(
                    pair_out.at[target], pair_in.at[m * Y + d - 1], ps_sem, pr_sem, (target, snd)
                ).start()

    hq = jnp.zeros((416, COLS), F32)
    for q in range(CHUNKS):
        columns = whole_flux(q)
        hq = hq + dot_nt(spread[0, q], columns) + dot_nt(spread[1, q], columns)
    hq_ref[...] = hq.astype(BF16)

    remote(pair_in, pair_in, ps_sem, pr_sem, opposite).wait_recv()
    own = pair_x[pl.ds(pl.multiple_of(cell * 8, 8), 8), :]
    pc_ref[...] = own + jnp.sum(pair_in[...].astype(F32), axis=0)

    finish()


def shards(
    footprint, spatial_cov, week_scale, band_width, sounding_weeks, target_print, target_weeks,
):
    hbm = pl.BlockSpec(memory_space=pltpu.HBM)
    vmem = pl.BlockSpec(memory_space=pltpu.VMEM)
    dma = pltpu.SemaphoreType.DMA
    hq, pair = pl.pallas_call(
        kernel,
        out_shape=(
            jax.ShapeDtypeStruct((416, COLS), BF16),
            jax.ShapeDtypeStruct((8, 128), F32),
        ),
        in_specs=[hbm] * 4 + [pl.BlockSpec(memory_space=pltpu.SMEM)] + [hbm] * 2,
        out_specs=(vmem, vmem),
        scratch_shapes=[
            pltpu.VMEM((CELLS, 4 * KC, 128), BF16),
            pltpu.VMEM((768, COLS), BF16),
            pltpu.VMEM((2, COLS, GROUP), BF16),
            pltpu.VMEM((256, 4, COLS), BF16),
            pltpu.VMEM((1024, COLS), BF16),
            pltpu.VMEM((1, 52), F32),
            pltpu.VMEM((1, 128), I32),
            pltpu.VMEM((1, 256), I32),
            pltpu.VMEM((CHUNKS, 1024, 256), F32),
            pltpu.VMEM((2, CHUNKS, 416, 256), BF16),
            pltpu.VMEM((CHUNKS, 2, COLS, 128), F32),
            pltpu.VMEM((CHUNKS, 2, X, SHARD, 128), BF16),
            pltpu.VMEM((len(PIECES), 2 * X - 1, HALF, 128), BF16),
            pltpu.VMEM((len(PIECES), HALF, 128), BF16),
            pltpu.VMEM((len(PIECES), HALF, 128), BF16),
            pltpu.VMEM((len(PIECES), HALF, 128), F32),
            pltpu.VMEM((CHUNKS, 2, X, SHARD, 128), BF16),
            pltpu.VMEM((TARGETS, 128), F32),
            pltpu.VMEM((CELLS, 8, 128), BF16),
            pltpu.VMEM((CELLS - 1, 8, 128), BF16),
            dma((6,)),
            dma, dma((CHUNKS, ZL - 1)),
            dma, dma((CHUNKS, 2)),
            dma((len(PIECES),)), dma((len(PIECES),)),
            dma((len(PIECES),)), dma((len(PIECES),)),
            dma((len(PIECES),)), dma((len(PIECES),)),
            dma, dma,
            pltpu.SemaphoreType.REGULAR,
        ],
        compiler_params=pltpu.CompilerParams(
            collective_id=0, has_side_effects=True, vmem_limit_bytes=48 << 20
        ),
        name="prior_products",
    )(
        in_hbm(jnp.transpose(footprint, (1, 2, 0)).reshape(4 * KC, 128)),
        in_hbm(spatial_cov),
        in_hbm(target_print),
        in_hbm(week_scale.reshape(1, 52)),
        band_width,
        in_hbm(sounding_weeks.reshape(1, 128)),
        in_hbm(target_weeks.reshape(1, 256)),
    )
    return jnp.transpose(hq.reshape(52, 8, COLS), (1, 0, 2)), pair.T


def solution(mesh):
    placed = (
        P(None, None, ("snd", "cells")),
        P("snd", "cells"),
        P(),
        P(),
        P(),
        P("snd", None, "cells"),
        P("snd"),
    )
    return jax.shard_map(
        shards,
        mesh=mesh,
        in_specs=placed,
        out_specs=(P("snd", None, "cells"), P(None, ("snd", "cells"))),
        check_vma=False,
    )
```

```python
import jax
import jax.numpy as jnp
from jax import lax
from jax.experimental import pallas as pl
from jax.experimental.pallas import tpu as pltpu
from jax.sharding import PartitionSpec as P

MESH = pl.DeviceIdType.MESH
F32, BF16, I32 = jnp.float32, jnp.bfloat16, jnp.int32
X, Y, ZL = 4, 4, 8
CELLS = 32
KC = 24
COLS = 384
SHARD = COLS // X
CHUNKS = 2
ROWS = 2 * KC
HALF = SHARD // 2
PIECES = [(q, h) for q in range(CHUNKS) for h in range(2)]
QUAD = ZL // 2
GROUP = Y * QUAD * KC
TARGETS = 256
AWAY = (1, 3, 2)
FAR_FIRST = (7, 6, 5, 4, 3, 2, 1)
HALF_LINE = (4, 3, 2, 1)


def iota(shape, dim):
    return lax.broadcasted_iota(I32, shape, dim)


def dot_nt(a, b, precision=None):
    return lax.dot_general(
        a, b, (((1,), (1,)), ((), ())), precision=precision, preferred_element_type=F32
    )


def dot_nn(a, b, precision=None):
    return lax.dot_general(
        a, b, (((1,), (0,)), ((), ())), precision=precision, preferred_element_type=F32
    )


def flip_bits(pos, mask):
    out = 0
    for bit in (0, 1, 2):
        value = (pos // (1 << bit)) % 2
        out = out + (1 << bit) * (1 - value if mask & (1 << bit) else value)
    return out


def in_hbm(array):
    return pltpu.with_memory_space_constraint(array, pltpu.HBM)


def kernel(
    f_hbm, c_hbm, g_hbm, scale_hbm, band_hbm, sw_hbm, tw_hbm,
    hq_ref, pc_ref,
    raw, c_buf, ct, g3, g2, scale_v, sw_v, tw_v, band_s,
    weights, spread, acc, sum_out, sum_in, z_out, z_in, z_own,
    flux, pair_x, pair_out, pair_in,
    load_sem, zs_sem, zr_sem, ys_sem, yr_sem, ss_sem, sr_sem,
    hs_sem, hr_sem, gs_sem, gr_sem, ps_sem, pr_sem, token,
):
    cell = lax.axis_index("cells")
    snd = lax.axis_index("snd")
    x, zh, core = snd // 4, (snd // 2) % 2, snd % 2
    y, zl = cell // ZL, cell % ZL

    def at_cells(yy, zz):
        return (yy * ZL + zz, snd)

    def at_snd(xx, hh, cc):
        return (cell, (xx * 2 + hh) * 2 + cc)

    def remote(src, dst, send, recv, device):
        return pltpu.make_async_remote_copy(
            src_ref=src, dst_ref=dst, send_sem=send, recv_sem=recv,
            device_id=device, device_id_type=MESH,
        )

    drains = []

    def finish():
        for drain in drains:
            drain()

    def later(ref, sem):
        drains.append(remote(ref, ref, sem, load_sem.at[0], opposite).wait_send)

    z_peer = {m: flip_bits(zl, m) for m in FAR_FIRST}
    y_peers = [(y + d) % Y for d in AWAY]
    sum_peers = [
        ((x + d) % X, (core + f) % 2) for d in (2, 1, 3, 0) for f in (0, 1) if d or f
    ]
    opposite = at_snd(x, 1 - zh, core)
    across = (y * ZL + z_peer[4], (x * 2 + 1 - zh) * 2 + core)

    barrier = pltpu.get_barrier_semaphore()
    greeted = [at_cells(y, z_peer[m]) for m in HALF_LINE] + [across]
    greeted += [at_cells(p, zl) for p in y_peers]
    greeted += [at_snd(xx, zh, cc) for xx, cc in sum_peers]
    for device in greeted:
        pl.semaphore_signal(barrier, inc=1, device_id=device, device_id_type=MESH)

    load_f = pltpu.make_async_copy(f_hbm, raw.at[cell], load_sem.at[0])
    load_f.start()
    loads = [
        pltpu.make_async_copy(src, dst, load_sem.at[1 + n])
        for n, (src, dst) in enumerate(
            (
                (scale_hbm, scale_v), (sw_hbm, sw_v), (tw_hbm, tw_v), (band_hbm, band_s),
                (c_hbm, c_buf), (g_hbm, g3),
            )
        )
    ]
    for copy in loads:
        copy.start()

    load_f.wait()
    pl.semaphore_wait(barrier, len(greeted))
    pl.semaphore_signal(token, inc=1, device_id=across, device_id_type=MESH)

    later(raw.at[pl.ds(0, ZL - 1)], zs_sem)
    later(raw.at[pl.ds(0, ZL * (Y - 1))], ys_sem)

    def piece(q, block):
        return raw.at[block, pl.ds(q * ROWS, ROWS)]

    def along_y(q, block, far):
        part = piece(q, block)
        for peer in y_peers:
            remote(part, part, ys_sem, yr_sem.at[q, far], at_cells(peer, zl)).start()

    def along_z(q, block, m, slot):
        part = piece(q, block)
        remote(
            part, part, zs_sem, zr_sem.at[q, slot - 1], at_cells(y, z_peer[m])
        ).start()

    def from_z(q, m):
        block = y * ZL + z_peer[m]
        part = piece(q, block)
        remote(part, part, zs_sem, zr_sem.at[q, m - 1], opposite).wait_recv()
        return block

    for q in range(CHUNKS):
        along_z(q, cell, 4, 4)
    for q in range(CHUNKS):
        for m in (1, 2, 3):
            along_z(q, cell, m, m)
        along_y(q, cell, 0)

    for copy in loads[:4]:
        copy.wait()
    top = lax.Precision.HIGHEST
    scale8 = jnp.broadcast_to(scale_v[...], (8, 52))
    eye = (iota((64, 52), 0) == iota((64, 52), 1)).astype(F32)
    scale_row = dot_nt(scale8, eye, top)
    scale_col = dot_nt(eye, scale8, top)
    lag = jnp.abs(iota((64, 64), 0) - iota((64, 64), 1))
    decay = jnp.exp(lag.astype(F32) * (-1.0 / 6.0))
    table = jnp.where(lag <= band_s[0, 0], decay, 0.0)
    table = table * scale_col[:, 0:1] * scale_row[0:1, :]
    first = sw_v[...]
    weeks = jnp.concatenate([first + a for a in range(4)], axis=1)
    source_pick = (iota((64, 512), 0) == weeks).astype(F32)
    source_rows = dot_nn(table, source_pick, top)
    row_hi = source_rows.astype(BF16)
    rest = source_rows - row_hi.astype(F32)
    row_mid = rest.astype(BF16)
    row_lo = (rest - row_mid.astype(F32)).astype(BF16)
    rows3 = jnp.concatenate([row_hi, row_mid, row_lo], axis=0)
    repeat = ((iota((1024, 256), 0) & 255) == iota((1024, 256), 1)).astype(BF16)
    target_first = jnp.broadcast_to(tw_v[...], (8, 256)).astype(F32).astype(BF16)
    target_col = dot_nt(repeat, target_first)[:, 0:1].astype(I32)
    target_week = target_col + (iota((1024, 1), 0) >> 8)
    target_pick = ((iota((1024, 192), 1) & 63) == target_week).astype(F32).astype(BF16)
    for q in range(CHUNKS):
        weights[q] = dot_nn(target_pick, rows3[:, q * 256 : (q + 1) * 256])
    loads[4].wait()
    for quad in range(2):
        rows = [
            c_buf[(g * 2 + quad) * QUAD * KC : (g * 2 + quad + 1) * QUAD * KC, :].astype(F32)
            for g in range(Y)
        ]
        ct[quad] = jnp.concatenate(rows, axis=0).T.astype(BF16)

    for q in range(CHUNKS):
        for m in (1, 4, 2, 3):
            block = from_z(q, m)
            if m == 4:
                for near in (1, 2, 3):
                    along_z(q, block, near, near + 4)
            along_y(q, block, m // 4)
    loads[5].wait()
    targets = g3[...].reshape(4 * TARGETS, COLS)
    offset = iota((TARGETS, 4 * TARGETS), 1) - 4 * iota((TARGETS, 4 * TARGETS), 0)
    for k in range(4):
        g2[k * TARGETS : (k + 1) * TARGETS] = dot_nn(
            (offset == k).astype(F32).astype(BF16), targets
        ).astype(BF16)

    for q in range(CHUNKS):
        for m in (5, 6, 7):
            along_y(q, from_z(q, m), 1)

    mine = (iota((8, 512), 1) & 127) == iota((8, 512), 0) + snd * 8
    mine = mine.astype(F32)
    wide = (source_rows[:52].reshape(52, 1, 512) * mine.reshape(1, 8, 512)).reshape(416, 512)
    wide_hi = wide.astype(BF16)
    wide_lo = (wide - wide_hi.astype(F32)).astype(BF16)
    for q in range(CHUNKS):
        spread[0, q] = wide_hi[:, q * 256 : (q + 1) * 256]
        spread[1, q] = wide_lo[:, q * 256 : (q + 1) * 256]

    def unpack(q, quad):
        blocks = [
            raw[pl.ds((g * 2 + quad) * QUAD, QUAD), q * ROWS : (q + 1) * ROWS].astype(F32)
            for g in range(Y)
        ]
        halves = [
            jnp.concatenate(
                [b[:, a * KC : (a + 1) * KC, :].reshape(QUAD * KC, 128) for b in blocks], axis=0
            ).astype(BF16)
            for a in range(2)
        ]
        return jnp.concatenate(halves, axis=1)

    own_quad = zl // QUAD

    def from_y(q, far):
        part = raw.at[pl.ds(0, QUAD * (Y - 1)), pl.ds(0, ROWS)]
        remote(part, part, ys_sem, yr_sem.at[q, far], opposite).wait_recv()

    def near_flux(q):
        from_y(q, 0)
        total = dot_nn(ct[own_quad], unpack(q, own_quad))
        for c in range(2):
            acc[q, c] = total[:, c * 128 : (c + 1) * 128]

    def partial_flux(q):
        from_y(q, 1)
        total = jnp.concatenate([acc[q, 0], acc[q, 1]], axis=1)
        total = total + dot_nn(ct[1 - own_quad], unpack(q, 1 - own_quad))
        for c in range(2):
            half = total[:, c * 128 : (c + 1) * 128]
            acc[q, c] = half
            sum_out[q, c] = half.astype(BF16).reshape(X, SHARD, 128)
        for h in range(2):
            p = 2 * q + h
            later(sum_in.at[p], ss_sem.at[p])
            for n, (xx, cc) in enumerate(sum_peers):
                remote(
                    sum_out.at[q, cc, xx, pl.ds(h * HALF, HALF)], sum_in.at[p, n],
                    ss_sem.at[p], sr_sem.at[p], at_snd(xx, zh, cc),
                ).start()

    def across_z(q, h):
        p = 2 * q + h
        every = sum_in.at[p]
        remote(every, every, ss_sem.at[p], sr_sem.at[p], opposite).wait_recv()
        rows = pl.ds(pl.multiple_of(x * SHARD + h * HALF, HALF), HALF)
        own = acc[q, core, rows, :] + jnp.sum(sum_in[p].astype(F32), axis=0)
        z_own[p] = own
        z_out[p] = own.astype(BF16)
        copy = remote(z_out.at[p], z_in.at[p], hs_sem.at[p], hr_sem.at[p], opposite)
        copy.start()
        drains.append(copy.wait_send)
        return copy

    def share(q, h, copy):
        p = 2 * q + h
        copy.wait_recv()
        flux[q, core, x, h * HALF : (h + 1) * HALF] = (z_own[p] + z_in[p].astype(F32)).astype(BF16)
        part = flux.at[q, core, x, pl.ds(h * HALF, HALF)]
        later(sum_in.at[p], gs_sem.at[p])
        for xx, cc in sum_peers:
            remote(part, part, gs_sem.at[p], gr_sem.at[p], at_snd(xx, zh, cc)).start()

    def whole_flux(q):
        return jnp.concatenate([flux[q, c].reshape(COLS, 128) for c in range(2)], axis=1)

    def products(q):
        for h in range(2):
            p = 2 * q + h
            every = sum_in.at[p]
            remote(every, every, gs_sem.at[p], gr_sem.at[p], opposite).wait_recv()
        both = dot_nn(g2[...], whole_flux(q)) * weights[q]
        both = both[:, :128] + both[:, 128:]
        return jnp.sum(both.reshape(4, TARGETS, 128), axis=0)

    for q in range(CHUNKS):
        near_flux(q)
    for q in range(CHUNKS):
        partial_flux(q)
    pl.semaphore_wait(token, 1)
    moved = [across_z(q, h) for q, h in PIECES]
    for q, h in PIECES:
        share(q, h, moved[2 * q + h])
    pair_x[...] = products(0)
    total = (pair_x[...] + products(1)).reshape(CELLS, 8, 128)
    pair_x[...] = total.reshape(TARGETS, 128)
    pair_out[...] = total.astype(BF16)

    later(pair_in, ps_sem)
    for d in (2, 1, 3, 0):
        for m in FAR_FIRST + (0,):
            if m or d:
                target = ((y + d) % Y) * ZL + (z_peer[m] if m else zl)
                remote(
                    pair_out.at[target], pair_in.at[m * Y + d - 1], ps_sem, pr_sem, (target, snd)
                ).start()

    hq = jnp.zeros((416, COLS), F32)
    for q in range(CHUNKS):
        columns = whole_flux(q)
        hq = hq + dot_nt(spread[0, q], columns) + dot_nt(spread[1, q], columns)
    hq_ref[...] = hq.astype(BF16)

    remote(pair_in, pair_in, ps_sem, pr_sem, opposite).wait_recv()
    own = pair_x[pl.ds(pl.multiple_of(cell * 8, 8), 8), :]
    pc_ref[...] = own + jnp.sum(pair_in[...].astype(F32), axis=0)

    finish()


def shards(
    footprint, spatial_cov, week_scale, band_width, sounding_weeks, target_print, target_weeks,
):
    hbm = pl.BlockSpec(memory_space=pltpu.HBM)
    vmem = pl.BlockSpec(memory_space=pltpu.VMEM)
    dma = pltpu.SemaphoreType.DMA
    hq, pair = pl.pallas_call(
        kernel,
        out_shape=(
            jax.ShapeDtypeStruct((416, COLS), BF16),
            jax.ShapeDtypeStruct((8, 128), F32),
        ),
        in_specs=[hbm] * 4 + [pl.BlockSpec(memory_space=pl.ANY)] + [hbm] * 2,
        out_specs=(vmem, vmem),
        scratch_shapes=[
            pltpu.VMEM((CELLS, 4 * KC, 128), BF16),
            pltpu.VMEM((768, COLS), BF16),
            pltpu.VMEM((2, COLS, GROUP), BF16),
            pltpu.VMEM((256, 4, COLS), BF16),
            pltpu.VMEM((1024, COLS), BF16),
            pltpu.VMEM((1, 52), F32),
            pltpu.VMEM((1, 128), I32),
            pltpu.VMEM((1, 256), I32),
            pltpu.SMEM((1, 1), I32),
            pltpu.VMEM((CHUNKS, 1024, 256), F32),
            pltpu.VMEM((2, CHUNKS, 416, 256), BF16),
            pltpu.VMEM((CHUNKS, 2, COLS, 128), F32),
            pltpu.VMEM((CHUNKS, 2, X, SHARD, 128), BF16),
            pltpu.VMEM((len(PIECES), 2 * X - 1, HALF, 128), BF16),
            pltpu.VMEM((len(PIECES), HALF, 128), BF16),
            pltpu.VMEM((len(PIECES), HALF, 128), BF16),
            pltpu.VMEM((len(PIECES), HALF, 128), F32),
            pltpu.VMEM((CHUNKS, 2, X, SHARD, 128), BF16),
            pltpu.VMEM((TARGETS, 128), F32),
            pltpu.VMEM((CELLS, 8, 128), BF16),
            pltpu.VMEM((CELLS - 1, 8, 128), BF16),
            dma((7,)),
            dma, dma((CHUNKS, ZL - 1)),
            dma, dma((CHUNKS, 2)),
            dma((len(PIECES),)), dma((len(PIECES),)),
            dma((len(PIECES),)), dma((len(PIECES),)),
            dma((len(PIECES),)), dma((len(PIECES),)),
            dma, dma,
            pltpu.SemaphoreType.REGULAR,
        ],
        compiler_params=pltpu.CompilerParams(
            collective_id=0, has_side_effects=True, vmem_limit_bytes=48 << 20
        ),
        name="prior_products",
    )(
        in_hbm(jnp.transpose(footprint, (1, 2, 0)).reshape(4 * KC, 128)),
        in_hbm(spatial_cov),
        in_hbm(target_print),
        in_hbm(week_scale.reshape(1, 52)),
        band_width.reshape(1, 1),
        in_hbm(sounding_weeks.reshape(1, 128)),
        in_hbm(target_weeks.reshape(1, 256)),
    )
    return jnp.transpose(hq.reshape(52, 8, COLS), (1, 0, 2)), pair.T


def solution(mesh):
    placed = (
        P(None, None, ("snd", "cells")),
        P("snd", "cells"),
        P(),
        P(),
        P(),
        P("snd", None, "cells"),
        P("snd"),
    )
    return jax.shard_map(
        shards,
        mesh=mesh,
        in_specs=placed,
        out_specs=(P("snd", None, "cells"), P(None, ("snd", "cells"))),
        check_vma=False,
    )
```

```python
import jax
import jax.numpy as jnp
from jax import lax
from jax.experimental import pallas as pl
from jax.experimental.pallas import tpu as pltpu
from jax.sharding import PartitionSpec as P

MESH = pl.DeviceIdType.MESH
F32, BF16, I32 = jnp.float32, jnp.bfloat16, jnp.int32
X, Y, ZL = 4, 4, 8
CELLS = 32
KC = 24
COLS = 384
SHARD = COLS // X
CHUNKS = 2
ROWS = 2 * KC
HALF = SHARD // 2
PIECES = [(q, h) for q in range(CHUNKS) for h in range(2)]
QUAD = ZL // 2
GROUP = Y * QUAD * KC
TARGETS = 256
AWAY = (1, 3, 2)
FAR_FIRST = (7, 6, 5, 4, 3, 2, 1)
HALF_LINE = (4, 3, 2, 1)


def iota(shape, dim):
    return lax.broadcasted_iota(I32, shape, dim)


def dot_nt(a, b, precision=None):
    return lax.dot_general(
        a, b, (((1,), (1,)), ((), ())), precision=precision, preferred_element_type=F32
    )


def dot_nn(a, b, precision=None):
    return lax.dot_general(
        a, b, (((1,), (0,)), ((), ())), precision=precision, preferred_element_type=F32
    )


def flip_bits(pos, mask):
    out = 0
    for bit in (0, 1, 2):
        value = (pos // (1 << bit)) % 2
        out = out + (1 << bit) * (1 - value if mask & (1 << bit) else value)
    return out


def in_hbm(array):
    return pltpu.with_memory_space_constraint(array, pltpu.HBM)


def kernel(
    f_hbm, c_hbm, g_hbm, scale_hbm, band_hbm, sw_hbm, tw_hbm,
    hq_ref, pc_ref,
    raw, c_buf, ct, g3, g2, scale_v, sw_v, tw_v, band_s,
    weights, acc, sum_out, sum_in, z_out, z_in, z_own,
    flux, pair_x, pair_out, pair_in,
    load_sem, zs_sem, zr_sem, ys_sem, yr_sem, ss_sem, sr_sem,
    hs_sem, hr_sem, gs_sem, gr_sem, ps_sem, pr_sem, token,
):
    cell = lax.axis_index("cells")
    snd = lax.axis_index("snd")
    x, zh, core = snd // 4, (snd // 2) % 2, snd % 2
    y, zl = cell // ZL, cell % ZL

    def at_cells(yy, zz):
        return (yy * ZL + zz, snd)

    def at_snd(xx, hh, cc):
        return (cell, (xx * 2 + hh) * 2 + cc)

    def remote(src, dst, send, recv, device):
        return pltpu.make_async_remote_copy(
            src_ref=src, dst_ref=dst, send_sem=send, recv_sem=recv,
            device_id=device, device_id_type=MESH,
        )

    drains = []

    def finish():
        for drain in drains:
            drain()

    def later(ref, sem):
        drains.append(remote(ref, ref, sem, load_sem.at[0], opposite).wait_send)

    z_peer = {m: flip_bits(zl, m) for m in FAR_FIRST}
    y_peers = [(y + d) % Y for d in AWAY]
    sum_peers = [
        ((x + d) % X, (core + f) % 2) for d in (2, 1, 3, 0) for f in (0, 1) if d or f
    ]
    opposite = at_snd(x, 1 - zh, core)
    across = (y * ZL + z_peer[4], (x * 2 + 1 - zh) * 2 + core)

    barrier = pltpu.get_barrier_semaphore()
    greeted = [at_cells(y, z_peer[m]) for m in HALF_LINE] + [across]
    greeted += [at_cells(p, zl) for p in y_peers]
    greeted += [at_snd(xx, zh, cc) for xx, cc in sum_peers]
    for device in greeted:
        pl.semaphore_signal(barrier, inc=1, device_id=device, device_id_type=MESH)

    load_f = pltpu.make_async_copy(f_hbm, raw.at[cell], load_sem.at[0])
    load_f.start()
    loads = [
        pltpu.make_async_copy(src, dst, load_sem.at[1 + n])
        for n, (src, dst) in enumerate(
            (
                (scale_hbm, scale_v), (sw_hbm, sw_v), (tw_hbm, tw_v), (band_hbm, band_s),
                (c_hbm, c_buf), (g_hbm, g3),
            )
        )
    ]
    for copy in loads:
        copy.start()

    load_f.wait()
    pl.semaphore_wait(barrier, len(greeted))
    pl.semaphore_signal(token, inc=1, device_id=across, device_id_type=MESH)

    later(raw.at[pl.ds(0, ZL - 1)], zs_sem)
    later(raw.at[pl.ds(0, ZL * (Y - 1))], ys_sem)

    def piece(q, block):
        return raw.at[block, pl.ds(q * ROWS, ROWS)]

    def along_y(q, block, far):
        part = piece(q, block)
        for peer in y_peers:
            remote(part, part, ys_sem, yr_sem.at[q, far], at_cells(peer, zl)).start()

    def along_z(q, block, m, slot):
        part = piece(q, block)
        remote(
            part, part, zs_sem, zr_sem.at[q, slot - 1], at_cells(y, z_peer[m])
        ).start()

    def from_z(q, m):
        block = y * ZL + z_peer[m]
        part = piece(q, block)
        remote(part, part, zs_sem, zr_sem.at[q, m - 1], opposite).wait_recv()
        return block

    for q in range(CHUNKS):
        along_z(q, cell, 4, 4)
    for q in range(CHUNKS):
        for m in (1, 2, 3):
            along_z(q, cell, m, m)
        along_y(q, cell, 0)

    for copy in loads[:4]:
        copy.wait()
    top = lax.Precision.HIGHEST
    scale8 = jnp.broadcast_to(scale_v[...], (8, 52))
    eye = (iota((64, 52), 0) == iota((64, 52), 1)).astype(F32)
    scale_row = dot_nt(scale8, eye, top)
    scale_col = dot_nt(eye, scale8, top)
    lag = jnp.abs(iota((64, 64), 0) - iota((64, 64), 1))
    decay = jnp.exp(lag.astype(F32) * (-1.0 / 6.0))
    table = jnp.where(lag <= band_s[0, 0], decay, 0.0)
    table = table * scale_col[:, 0:1] * scale_row[0:1, :]
    first = sw_v[...]
    weeks = jnp.concatenate([first + a for a in range(4)], axis=1)
    source_pick = (iota((64, 512), 0) == weeks).astype(F32)
    source_rows = dot_nn(table, source_pick, top)
    row_hi = source_rows.astype(BF16)
    rest = source_rows - row_hi.astype(F32)
    row_mid = rest.astype(BF16)
    row_lo = (rest - row_mid.astype(F32)).astype(BF16)
    rows3 = jnp.concatenate([row_hi, row_mid, row_lo], axis=0)
    repeat = ((iota((1024, 256), 0) & 255) == iota((1024, 256), 1)).astype(BF16)
    target_first = jnp.broadcast_to(tw_v[...], (8, 256)).astype(F32).astype(BF16)
    target_col = dot_nt(repeat, target_first)[:, 0:1].astype(I32)
    target_week = target_col + (iota((1024, 1), 0) >> 8)
    target_pick = ((iota((1024, 192), 1) & 63) == target_week).astype(F32).astype(BF16)
    for q in range(CHUNKS):
        weights[q] = dot_nn(target_pick, rows3[:, q * 256 : (q + 1) * 256])
    loads[4].wait()
    for quad in range(2):
        rows = [
            c_buf[(g * 2 + quad) * QUAD * KC : (g * 2 + quad + 1) * QUAD * KC, :].astype(F32)
            for g in range(Y)
        ]
        ct[quad] = jnp.concatenate(rows, axis=0).T.astype(BF16)

    for q in range(CHUNKS):
        for m in (1, 4, 2, 3):
            block = from_z(q, m)
            if m == 4:
                for near in (1, 2, 3):
                    along_z(q, block, near, near + 4)
            along_y(q, block, m // 4)
    loads[5].wait()
    targets = g3[...].reshape(4 * TARGETS, COLS)
    offset = iota((TARGETS, 4 * TARGETS), 1) - 4 * iota((TARGETS, 4 * TARGETS), 0)
    for k in range(4):
        g2[k * TARGETS : (k + 1) * TARGETS] = dot_nn(
            (offset == k).astype(F32).astype(BF16), targets
        ).astype(BF16)

    def unpack(q, quad):
        blocks = [
            raw[pl.ds((g * 2 + quad) * QUAD, QUAD), q * ROWS : (q + 1) * ROWS].astype(F32)
            for g in range(Y)
        ]
        halves = [
            jnp.concatenate(
                [b[:, a * KC : (a + 1) * KC, :].reshape(QUAD * KC, 128) for b in blocks], axis=0
            ).astype(BF16)
            for a in range(2)
        ]
        return jnp.concatenate(halves, axis=1)

    own_quad = zl // QUAD

    def from_y(q, far):
        part = raw.at[pl.ds(0, QUAD * (Y - 1)), pl.ds(0, ROWS)]
        remote(part, part, ys_sem, yr_sem.at[q, far], opposite).wait_recv()

    def near_flux(q):
        from_y(q, 0)
        total = dot_nn(ct[own_quad], unpack(q, own_quad))
        for c in range(2):
            acc[q, c] = total[:, c * 128 : (c + 1) * 128]

    def partial_flux(q):
        from_y(q, 1)
        total = jnp.concatenate([acc[q, 0], acc[q, 1]], axis=1)
        total = total + dot_nn(ct[1 - own_quad], unpack(q, 1 - own_quad))
        for c in range(2):
            half = total[:, c * 128 : (c + 1) * 128]
            acc[q, c] = half
            sum_out[q, c] = half.astype(BF16).reshape(X, SHARD, 128)
        for h in range(2):
            p = 2 * q + h
            later(sum_in.at[p], ss_sem.at[p])
            for n, (xx, cc) in enumerate(sum_peers):
                remote(
                    sum_out.at[q, cc, xx, pl.ds(h * HALF, HALF)], sum_in.at[p, n],
                    ss_sem.at[p], sr_sem.at[p], at_snd(xx, zh, cc),
                ).start()

    def across_z(q, h):
        p = 2 * q + h
        every = sum_in.at[p]
        remote(every, every, ss_sem.at[p], sr_sem.at[p], opposite).wait_recv()
        rows = pl.ds(pl.multiple_of(x * SHARD + h * HALF, HALF), HALF)
        own = acc[q, core, rows, :] + jnp.sum(sum_in[p].astype(F32), axis=0)
        z_own[p] = own
        z_out[p] = own.astype(BF16)
        copy = remote(z_out.at[p], z_in.at[p], hs_sem.at[p], hr_sem.at[p], opposite)
        copy.start()
        drains.append(copy.wait_send)
        return copy

    def share(q, h, copy):
        p = 2 * q + h
        copy.wait_recv()
        flux[q, core, x, h * HALF : (h + 1) * HALF] = (z_own[p] + z_in[p].astype(F32)).astype(BF16)
        part = flux.at[q, core, x, pl.ds(h * HALF, HALF)]
        later(sum_in.at[p], gs_sem.at[p])
        for xx, cc in sum_peers:
            remote(part, part, gs_sem.at[p], gr_sem.at[p], at_snd(xx, zh, cc)).start()

    def whole_flux(q):
        return jnp.concatenate([flux[q, c].reshape(COLS, 128) for c in range(2)], axis=1)

    def products(q):
        for h in range(2):
            p = 2 * q + h
            every = sum_in.at[p]
            remote(every, every, gs_sem.at[p], gr_sem.at[p], opposite).wait_recv()
        both = dot_nn(g2[...], whole_flux(q)) * weights[q]
        both = both[:, :128] + both[:, 128:]
        return jnp.sum(both.reshape(4, TARGETS, 128), axis=0)

    for q in range(CHUNKS):
        for m in (5, 6, 7):
            along_y(q, from_z(q, m), 1)
        near_flux(q)
    for q in range(CHUNKS):
        partial_flux(q)
    pl.semaphore_wait(token, 1)
    moved = [across_z(q, h) for q, h in PIECES]
    for q, h in PIECES:
        share(q, h, moved[2 * q + h])
    pair_x[...] = products(0)
    total = (pair_x[...] + products(1)).reshape(CELLS, 8, 128)
    pair_x[...] = total.reshape(TARGETS, 128)
    pair_out[...] = total.astype(BF16)

    for d in (2, 1, 3, 0):
        for m in FAR_FIRST + (0,):
            if m or d:
                target = ((y + d) % Y) * ZL + (z_peer[m] if m else zl)
                remote(
                    pair_out.at[target], pair_in.at[m * Y + d - 1], ps_sem, pr_sem, (target, snd)
                ).start()

    mine = (iota((8, 512), 1) & 127) == iota((8, 512), 0) + snd * 8
    mine = mine.astype(F32)
    wide = (source_rows[:52].reshape(52, 1, 512) * mine.reshape(1, 8, 512)).reshape(416, 512)
    wide_hi = wide.astype(BF16)
    wide_lo = (wide - wide_hi.astype(F32)).astype(BF16)
    hq = jnp.zeros((416, COLS), F32)
    for q in range(CHUNKS):
        columns = whole_flux(q)
        lanes = slice(q * 256, (q + 1) * 256)
        hq = hq + dot_nt(wide_hi[:, lanes], columns) + dot_nt(wide_lo[:, lanes], columns)
    hq_ref[...] = hq.astype(BF16)

    finish()
    last = remote(pair_in, pair_in, ps_sem, pr_sem, opposite)
    last.wait_recv()
    own = pair_x[pl.ds(pl.multiple_of(cell * 8, 8), 8), :]
    pc_ref[...] = own + jnp.sum(pair_in[...].astype(F32), axis=0)

    last.wait_send()


def shards(
    footprint, spatial_cov, week_scale, band_width, sounding_weeks, target_print, target_weeks,
):
    hbm = pl.BlockSpec(memory_space=pltpu.HBM)
    vmem = pl.BlockSpec(memory_space=pltpu.VMEM)
    dma = pltpu.SemaphoreType.DMA
    hq, pair = pl.pallas_call(
        kernel,
        out_shape=(
            jax.ShapeDtypeStruct((416, COLS), BF16),
            jax.ShapeDtypeStruct((8, 128), F32),
        ),
        in_specs=[hbm] * 4 + [pl.BlockSpec(memory_space=pl.ANY)] + [hbm] * 2,
        out_specs=(vmem, vmem),
        scratch_shapes=[
            pltpu.VMEM((CELLS, 4 * KC, 128), BF16),
            pltpu.VMEM((768, COLS), BF16),
            pltpu.VMEM((2, COLS, GROUP), BF16),
            pltpu.VMEM((256, 4, COLS), BF16),
            pltpu.VMEM((1024, COLS), BF16),
            pltpu.VMEM((1, 52), F32),
            pltpu.VMEM((1, 128), I32),
            pltpu.VMEM((1, 256), I32),
            pltpu.SMEM((1, 1), I32),
            pltpu.VMEM((CHUNKS, 1024, 256), F32),
            pltpu.VMEM((CHUNKS, 2, COLS, 128), F32),
            pltpu.VMEM((CHUNKS, 2, X, SHARD, 128), BF16),
            pltpu.VMEM((len(PIECES), 2 * X - 1, HALF, 128), BF16),
            pltpu.VMEM((len(PIECES), HALF, 128), BF16),
            pltpu.VMEM((len(PIECES), HALF, 128), BF16),
            pltpu.VMEM((len(PIECES), HALF, 128), F32),
            pltpu.VMEM((CHUNKS, 2, X, SHARD, 128), BF16),
            pltpu.VMEM((TARGETS, 128), F32),
            pltpu.VMEM((CELLS, 8, 128), BF16),
            pltpu.VMEM((CELLS - 1, 8, 128), BF16),
            dma((7,)),
            dma, dma((CHUNKS, ZL - 1)),
            dma, dma((CHUNKS, 2)),
            dma((len(PIECES),)), dma((len(PIECES),)),
            dma((len(PIECES),)), dma((len(PIECES),)),
            dma((len(PIECES),)), dma((len(PIECES),)),
            dma, dma,
            pltpu.SemaphoreType.REGULAR,
        ],
        compiler_params=pltpu.CompilerParams(
            collective_id=0, has_side_effects=True, vmem_limit_bytes=48 << 20
        ),
        name="prior_products",
    )(
        in_hbm(jnp.transpose(footprint, (1, 2, 0)).reshape(4 * KC, 128)),
        in_hbm(spatial_cov),
        in_hbm(target_print),
        in_hbm(week_scale.reshape(1, 52)),
        band_width.reshape(1, 1),
        in_hbm(sounding_weeks.reshape(1, 128)),
        in_hbm(target_weeks.reshape(1, 256)),
    )
    return jnp.transpose(hq.reshape(52, 8, COLS), (1, 0, 2)), pair.T


def solution(mesh):
    placed = (
        P(None, None, ("snd", "cells")),
        P("snd", "cells"),
        P(),
        P(),
        P(),
        P("snd", None, "cells"),
        P("snd"),
    )
    return jax.shard_map(
        shards,
        mesh=mesh,
        in_specs=placed,
        out_specs=(P("snd", None, "cells"), P(None, ("snd", "cells"))),
        check_vma=False,
    )
```

```python
import jax
import jax.numpy as jnp
from jax import lax
from jax.experimental import pallas as pl
from jax.experimental.pallas import tpu as pltpu
from jax.sharding import PartitionSpec as P

MESH = pl.DeviceIdType.MESH
F32, BF16, I32 = jnp.float32, jnp.bfloat16, jnp.int32
X, Y, ZL = 4, 4, 8
CELLS = 32
KC = 24
COLS = 384
SHARD = COLS // X
CHUNKS = 2
ROWS = 2 * KC
HALF = SHARD // 2
PIECES = [(q, h) for q in range(CHUNKS) for h in range(2)]
QUAD = ZL // 2
GROUP = Y * QUAD * KC
TARGETS = 256
AWAY = (1, 3, 2)
FAR_FIRST = (7, 6, 5, 4, 3, 2, 1)
HALF_LINE = (4, 3, 2, 1)


def iota(shape, dim):
    return lax.broadcasted_iota(I32, shape, dim)


def dot_nt(a, b, precision=None):
    return lax.dot_general(
        a, b, (((1,), (1,)), ((), ())), precision=precision, preferred_element_type=F32
    )


def dot_nn(a, b, precision=None):
    return lax.dot_general(
        a, b, (((1,), (0,)), ((), ())), precision=precision, preferred_element_type=F32
    )


def flip_bits(pos, mask):
    out = 0
    for bit in (0, 1, 2):
        value = (pos // (1 << bit)) % 2
        out = out + (1 << bit) * (1 - value if mask & (1 << bit) else value)
    return out


def in_hbm(array):
    return pltpu.with_memory_space_constraint(array, pltpu.HBM)


def kernel(
    f_hbm, c_hbm, g_hbm, scale_hbm, band_hbm, sw_hbm, tw_hbm,
    hq_ref, pc_ref,
    raw, c_buf, ct, g3, g2, scale_v, sw_v, tw_v, band_s,
    weights, acc, sum_out, sum_in, z_out, z_in, z_own,
    flux, pair_x, pair_out, pair_in,
    load_sem, zs_sem, zr_sem, ys_sem, yr_sem, ss_sem, sr_sem,
    hs_sem, hr_sem, gs_sem, gr_sem, ps_sem, pr_sem, token,
):
    cell = lax.axis_index("cells")
    snd = lax.axis_index("snd")
    x, zh, core = snd // 4, (snd // 2) % 2, snd % 2
    y, zl = cell // ZL, cell % ZL

    def at_cells(yy, zz):
        return (yy * ZL + zz, snd)

    def at_snd(xx, hh, cc):
        return (cell, (xx * 2 + hh) * 2 + cc)

    def remote(src, dst, send, recv, device):
        return pltpu.make_async_remote_copy(
            src_ref=src, dst_ref=dst, send_sem=send, recv_sem=recv,
            device_id=device, device_id_type=MESH,
        )

    drains = []

    def finish():
        for drain in drains:
            drain()

    def later(ref, sem):
        drains.append(remote(ref, ref, sem, load_sem.at[0], opposite).wait_send)

    z_peer = {m: flip_bits(zl, m) for m in FAR_FIRST}
    y_peers = [(y + d) % Y for d in AWAY]
    sum_peers = [
        ((x + d) % X, (core + f) % 2) for d in (2, 1, 3, 0) for f in (0, 1) if d or f
    ]
    opposite = at_snd(x, 1 - zh, core)
    across = (y * ZL + z_peer[4], (x * 2 + 1 - zh) * 2 + core)

    barrier = pltpu.get_barrier_semaphore()
    greeted = [at_cells(y, z_peer[m]) for m in HALF_LINE] + [across]
    greeted += [at_cells(p, zl) for p in y_peers]
    greeted += [at_snd(xx, zh, cc) for xx, cc in sum_peers]
    for device in greeted:
        pl.semaphore_signal(barrier, inc=1, device_id=device, device_id_type=MESH)

    load_f = pltpu.make_async_copy(f_hbm, raw.at[cell], load_sem.at[0])
    load_f.start()
    loads = [
        pltpu.make_async_copy(src, dst, load_sem.at[1 + n])
        for n, (src, dst) in enumerate(
            (
                (scale_hbm, scale_v), (sw_hbm, sw_v), (tw_hbm, tw_v), (band_hbm, band_s),
                (c_hbm, c_buf), (g_hbm, g3),
            )
        )
    ]
    for copy in loads:
        copy.start()

    load_f.wait()
    pl.semaphore_wait(barrier, len(greeted))
    pl.semaphore_signal(token, inc=1, device_id=across, device_id_type=MESH)

    later(raw.at[pl.ds(0, ZL - 1)], zs_sem)
    later(raw.at[pl.ds(0, ZL * (Y - 1))], ys_sem)

    def piece(q, block):
        return raw.at[block, pl.ds(q * ROWS, ROWS)]

    def along_y(q, block, far):
        part = piece(q, block)
        for peer in y_peers:
            remote(part, part, ys_sem, yr_sem.at[q, far], at_cells(peer, zl)).start()

    def along_z(q, block, m, slot):
        part = piece(q, block)
        remote(
            part, part, zs_sem, zr_sem.at[q, slot - 1], at_cells(y, z_peer[m])
        ).start()

    def from_z(q, m):
        block = y * ZL + z_peer[m]
        part = piece(q, block)
        remote(part, part, zs_sem, zr_sem.at[q, m - 1], opposite).wait_recv()
        return block

    for q in range(CHUNKS):
        along_z(q, cell, 4, 4)
    for q in range(CHUNKS):
        for m in (1, 2, 3):
            along_z(q, cell, m, m)
        along_y(q, cell, 0)

    for copy in loads[:4]:
        copy.wait()
    top = lax.Precision.HIGHEST
    scale8 = jnp.broadcast_to(scale_v[...], (8, 52))
    eye = (iota((64, 52), 0) == iota((64, 52), 1)).astype(F32)
    scale_row = dot_nt(scale8, eye, top)
    scale_col = dot_nt(eye, scale8, top)
    lag = jnp.abs(iota((64, 64), 0) - iota((64, 64), 1))
    decay = jnp.exp(lag.astype(F32) * (-1.0 / 6.0))
    table = jnp.where(lag <= band_s[0, 0], decay, 0.0)
    table = table * scale_col[:, 0:1] * scale_row[0:1, :]
    first = sw_v[...]
    weeks = jnp.concatenate([first + a for a in range(4)], axis=1)
    source_pick = (iota((64, 512), 0) == weeks).astype(F32)
    source_rows = dot_nn(table, source_pick, top)
    row_hi = source_rows.astype(BF16)
    rest = source_rows - row_hi.astype(F32)
    row_mid = rest.astype(BF16)
    row_lo = (rest - row_mid.astype(F32)).astype(BF16)
    rows3 = jnp.concatenate([row_hi, row_mid, row_lo], axis=0)
    repeat = ((iota((1024, 256), 0) & 255) == iota((1024, 256), 1)).astype(BF16)
    target_first = jnp.broadcast_to(tw_v[...], (8, 256)).astype(F32).astype(BF16)
    target_col = dot_nt(repeat, target_first)[:, 0:1].astype(I32)
    target_week = target_col + (iota((1024, 1), 0) >> 8)
    target_pick = ((iota((1024, 192), 1) & 63) == target_week).astype(F32).astype(BF16)
    for q in range(CHUNKS):
        weights[q] = dot_nn(target_pick, rows3[:, q * 256 : (q + 1) * 256])
    loads[4].wait()
    for quad in range(2):
        rows = [
            c_buf[(g * 2 + quad) * QUAD * KC : (g * 2 + quad + 1) * QUAD * KC, :].astype(F32)
            for g in range(Y)
        ]
        ct[quad] = jnp.concatenate(rows, axis=0).T.astype(BF16)

    for q in range(CHUNKS):
        for m in (1, 4, 2, 3):
            block = from_z(q, m)
            if m == 4:
                for near in (1, 2, 3):
                    along_z(q, block, near, near + 4)
            along_y(q, block, m // 4)
    loads[5].wait()
    targets = g3[...].reshape(4 * TARGETS, COLS)
    offset = iota((TARGETS, 4 * TARGETS), 1) - 4 * iota((TARGETS, 4 * TARGETS), 0)
    for k in range(4):
        g2[k * TARGETS : (k + 1) * TARGETS] = dot_nn(
            (offset == k).astype(F32).astype(BF16), targets
        ).astype(BF16)

    def unpack(q, quad):
        blocks = [
            raw[pl.ds((g * 2 + quad) * QUAD, QUAD), q * ROWS : (q + 1) * ROWS].astype(F32)
            for g in range(Y)
        ]
        halves = [
            jnp.concatenate(
                [b[:, a * KC : (a + 1) * KC, :].reshape(QUAD * KC, 128) for b in blocks], axis=0
            ).astype(BF16)
            for a in range(2)
        ]
        return jnp.concatenate(halves, axis=1)

    own_quad = zl // QUAD

    def from_y(q, far):
        part = raw.at[pl.ds(0, QUAD * (Y - 1)), pl.ds(0, ROWS)]
        remote(part, part, ys_sem, yr_sem.at[q, far], opposite).wait_recv()

    def near_flux(q):
        from_y(q, 0)
        total = dot_nn(ct[own_quad], unpack(q, own_quad))
        for c in range(2):
            acc[q, c] = total[:, c * 128 : (c + 1) * 128]

    def partial_flux(q):
        from_y(q, 1)
        total = jnp.concatenate([acc[q, 0], acc[q, 1]], axis=1)
        total = total + dot_nn(ct[1 - own_quad], unpack(q, 1 - own_quad))
        for c in range(2):
            half = total[:, c * 128 : (c + 1) * 128]
            acc[q, c] = half
            sum_out[q, c] = half.astype(BF16).reshape(X, SHARD, 128)
        for h in range(2):
            p = 2 * q + h
            later(sum_in.at[p], ss_sem.at[p])
            for n, (xx, cc) in enumerate(sum_peers):
                remote(
                    sum_out.at[q, cc, xx, pl.ds(h * HALF, HALF)], sum_in.at[p, n],
                    ss_sem.at[p], sr_sem.at[p], at_snd(xx, zh, cc),
                ).start()

    def across_z(q, h):
        p = 2 * q + h
        every = sum_in.at[p]
        remote(every, every, ss_sem.at[p], sr_sem.at[p], opposite).wait_recv()
        rows = pl.ds(pl.multiple_of(x * SHARD + h * HALF, HALF), HALF)
        own = acc[q, core, rows, :] + jnp.sum(sum_in[p].astype(F32), axis=0)
        z_own[p] = own
        z_out[p] = own.astype(BF16)
        copy = remote(z_out.at[p], z_in.at[p], hs_sem.at[p], hr_sem.at[p], opposite)
        copy.start()
        drains.append(copy.wait_send)
        return copy

    def share(q, h, copy):
        p = 2 * q + h
        copy.wait_recv()
        flux[q, core, x, h * HALF : (h + 1) * HALF] = (z_own[p] + z_in[p].astype(F32)).astype(BF16)
        part = flux.at[q, core, x, pl.ds(h * HALF, HALF)]
        later(sum_in.at[p], gs_sem.at[p])
        for xx, cc in sum_peers:
            remote(part, part, gs_sem.at[p], gr_sem.at[p], at_snd(xx, zh, cc)).start()

    def whole_flux(q):
        return jnp.concatenate([flux[q, c].reshape(COLS, 128) for c in range(2)], axis=1)

    def products(q):
        for h in range(2):
            p = 2 * q + h
            every = sum_in.at[p]
            remote(every, every, gs_sem.at[p], gr_sem.at[p], opposite).wait_recv()
        both = dot_nn(g2[...], whole_flux(q)) * weights[q]
        both = both[:, :128] + both[:, 128:]
        return jnp.sum(both.reshape(4, TARGETS, 128), axis=0)

    for q in range(CHUNKS):
        for m in (5, 6, 7):
            along_y(q, from_z(q, m), 1)
    for q in range(CHUNKS):
        near_flux(q)
    for q in range(CHUNKS):
        partial_flux(q)
    pl.semaphore_wait(token, 1)
    moved = [across_z(q, h) for q, h in PIECES]
    for q, h in PIECES:
        share(q, h, moved[2 * q + h])
    pair_x[...] = products(0)
    total = (pair_x[...] + products(1)).reshape(CELLS, 8, 128)
    pair_x[...] = total.reshape(TARGETS, 128)
    pair_out[...] = total.astype(BF16)

    for d in (2, 1, 3, 0):
        for m in FAR_FIRST + (0,):
            if m or d:
                target = ((y + d) % Y) * ZL + (z_peer[m] if m else zl)
                remote(
                    pair_out.at[target], pair_in.at[m * Y + d - 1], ps_sem, pr_sem, (target, snd)
                ).start()

    mine = (iota((8, 512), 1) & 127) == iota((8, 512), 0) + snd * 8
    mine = mine.astype(F32)
    wide = (source_rows[:52].reshape(52, 1, 512) * mine.reshape(1, 8, 512)).reshape(416, 512)
    wide_hi = wide.astype(BF16)
    wide_lo = (wide - wide_hi.astype(F32)).astype(BF16)
    hq = jnp.zeros((416, COLS), F32)
    for q in range(CHUNKS):
        columns = whole_flux(q)
        lanes = slice(q * 256, (q + 1) * 256)
        hq = hq + dot_nt(wide_hi[:, lanes], columns) + dot_nt(wide_lo[:, lanes], columns)
    hq_ref[...] = hq.astype(BF16)

    finish()
    last = remote(pair_in, pair_in, ps_sem, pr_sem, opposite)
    last.wait_recv()
    own = pair_x[pl.ds(pl.multiple_of(cell * 8, 8), 8), :]
    pc_ref[...] = own + jnp.sum(pair_in[...].astype(F32), axis=0)

    last.wait_send()


def shards(
    footprint, spatial_cov, week_scale, band_width, sounding_weeks, target_print, target_weeks,
):
    hbm = pl.BlockSpec(memory_space=pltpu.HBM)
    vmem = pl.BlockSpec(memory_space=pltpu.VMEM)
    dma = pltpu.SemaphoreType.DMA
    hq, pair = pl.pallas_call(
        kernel,
        out_shape=(
            jax.ShapeDtypeStruct((416, COLS), BF16),
            jax.ShapeDtypeStruct((8, 128), F32),
        ),
        in_specs=[hbm] * 4 + [pl.BlockSpec(memory_space=pl.ANY)] + [hbm] * 2,
        out_specs=(vmem, vmem),
        scratch_shapes=[
            pltpu.VMEM((CELLS, 4 * KC, 128), BF16),
            pltpu.VMEM((768, COLS), BF16),
            pltpu.VMEM((2, COLS, GROUP), BF16),
            pltpu.VMEM((256, 4, COLS), BF16),
            pltpu.VMEM((1024, COLS), BF16),
            pltpu.VMEM((1, 52), F32),
            pltpu.VMEM((1, 128), I32),
            pltpu.VMEM((1, 256), I32),
            pltpu.SMEM((1, 1), I32),
            pltpu.VMEM((CHUNKS, 1024, 256), F32),
            pltpu.VMEM((CHUNKS, 2, COLS, 128), F32),
            pltpu.VMEM((CHUNKS, 2, X, SHARD, 128), BF16),
            pltpu.VMEM((len(PIECES), 2 * X - 1, HALF, 128), BF16),
            pltpu.VMEM((len(PIECES), HALF, 128), BF16),
            pltpu.VMEM((len(PIECES), HALF, 128), BF16),
            pltpu.VMEM((len(PIECES), HALF, 128), F32),
            pltpu.VMEM((CHUNKS, 2, X, SHARD, 128), BF16),
            pltpu.VMEM((TARGETS, 128), F32),
            pltpu.VMEM((CELLS, 8, 128), BF16),
            pltpu.VMEM((CELLS - 1, 8, 128), BF16),
            dma((7,)),
            dma, dma((CHUNKS, ZL - 1)),
            dma, dma((CHUNKS, 2)),
            dma((len(PIECES),)), dma((len(PIECES),)),
            dma((len(PIECES),)), dma((len(PIECES),)),
            dma((len(PIECES),)), dma((len(PIECES),)),
            dma, dma,
            pltpu.SemaphoreType.REGULAR,
        ],
        compiler_params=pltpu.CompilerParams(
            collective_id=0, has_side_effects=True, vmem_limit_bytes=48 << 20
        ),
        name="prior_products",
    )(
        in_hbm(jnp.transpose(footprint, (1, 2, 0)).reshape(4 * KC, 128)),
        in_hbm(spatial_cov),
        in_hbm(target_print),
        in_hbm(week_scale.reshape(1, 52)),
        band_width.reshape(1, 1),
        in_hbm(sounding_weeks.reshape(1, 128)),
        in_hbm(target_weeks.reshape(1, 256)),
    )
    return jnp.transpose(hq.reshape(52, 8, COLS), (1, 0, 2)), pair.T


def solution(mesh):
    placed = (
        P(None, None, ("snd", "cells")),
        P("snd", "cells"),
        P(),
        P(),
        P(),
        P("snd", None, "cells"),
        P("snd"),
    )
    return jax.shard_map(
        shards,
        mesh=mesh,
        in_specs=placed,
        out_specs=(P("snd", None, "cells"), P(None, ("snd", "cells"))),
        check_vma=False,
    )
```

```python
import jax
import jax.numpy as jnp
from jax import lax
from jax.experimental import pallas as pl
from jax.experimental.pallas import tpu as pltpu
from jax.sharding import PartitionSpec as P

MESH = pl.DeviceIdType.MESH
F32, BF16, I32 = jnp.float32, jnp.bfloat16, jnp.int32
X, Y, ZL = 4, 4, 8
CELLS = 32
KC = 24
COLS = 384
SHARD = COLS // X
CHUNKS = 2
ROWS = 2 * KC
HALF = SHARD // 2
PIECES = [(q, h) for q in range(CHUNKS) for h in range(2)]
QUAD = ZL // 2
GROUP = Y * QUAD * KC
TARGETS = 256
AWAY = (2, 1, 3)
FAR_FIRST = (7, 6, 5, 4, 3, 2, 1)
HALF_LINE = (4, 3, 2, 1)


def iota(shape, dim):
    return lax.broadcasted_iota(I32, shape, dim)


def dot_nt(a, b, precision=None):
    return lax.dot_general(
        a, b, (((1,), (1,)), ((), ())), precision=precision, preferred_element_type=F32
    )


def dot_nn(a, b, precision=None):
    return lax.dot_general(
        a, b, (((1,), (0,)), ((), ())), precision=precision, preferred_element_type=F32
    )


def flip_bits(pos, mask):
    out = 0
    for bit in (0, 1, 2):
        value = (pos // (1 << bit)) % 2
        out = out + (1 << bit) * (1 - value if mask & (1 << bit) else value)
    return out


def in_hbm(array):
    return pltpu.with_memory_space_constraint(array, pltpu.HBM)


def kernel(
    f_hbm, c_hbm, g_hbm, scale_hbm, band_hbm, sw_hbm, tw_hbm,
    hq_ref, pc_ref,
    raw, c_buf, ct, g3, g2, scale_v, sw_v, tw_v, band_s,
    weights, spread, acc, sum_out, sum_in, z_out, z_in, z_own,
    flux, pair_x, pair_out, pair_in,
    load_sem, zs_sem, zr_sem, ys_sem, yr_sem, ss_sem, sr_sem,
    hs_sem, hr_sem, gs_sem, gr_sem, ps_sem, pr_sem, token,
):
    cell = lax.axis_index("cells")
    snd = lax.axis_index("snd")
    x, zh, core = snd // 4, (snd // 2) % 2, snd % 2
    y, zl = cell // ZL, cell % ZL

    def at_cells(yy, zz):
        return (yy * ZL + zz, snd)

    def at_snd(xx, hh, cc):
        return (cell, (xx * 2 + hh) * 2 + cc)

    def remote(src, dst, send, recv, device):
        return pltpu.make_async_remote_copy(
            src_ref=src, dst_ref=dst, send_sem=send, recv_sem=recv,
            device_id=device, device_id_type=MESH,
        )

    drains = []

    def finish():
        for drain in drains:
            drain()

    def later(ref, sem):
        drains.append(remote(ref, ref, sem, load_sem.at[0], opposite).wait_send)

    z_peer = {m: flip_bits(zl, m) for m in FAR_FIRST}
    y_peers = [(y + d) % Y for d in AWAY]
    sum_peers = [
        ((x + d) % X, (core + f) % 2) for d in (2, 1, 3, 0) for f in (0, 1) if d or f
    ]
    opposite = at_snd(x, 1 - zh, core)
    across = (y * ZL + z_peer[4], (x * 2 + 1 - zh) * 2 + core)

    barrier = pltpu.get_barrier_semaphore()
    greeted = [at_cells(y, z_peer[m]) for m in HALF_LINE] + [across]
    greeted += [at_cells(p, zl) for p in y_peers]
    greeted += [at_snd(xx, zh, cc) for xx, cc in sum_peers]
    for device in greeted:
        pl.semaphore_signal(barrier, inc=1, device_id=device, device_id_type=MESH)

    load_f = pltpu.make_async_copy(f_hbm, raw.at[cell], load_sem.at[0])
    load_f.start()
    loads = [
        pltpu.make_async_copy(src, dst, load_sem.at[1 + n])
        for n, (src, dst) in enumerate(
            (
                (scale_hbm, scale_v), (sw_hbm, sw_v), (tw_hbm, tw_v), (band_hbm, band_s),
                (c_hbm, c_buf), (g_hbm, g3),
            )
        )
    ]
    for copy in loads:
        copy.start()

    load_f.wait()
    pl.semaphore_wait(barrier, len(greeted))
    pl.semaphore_signal(token, inc=1, device_id=across, device_id_type=MESH)

    later(raw.at[pl.ds(0, ZL - 1)], zs_sem)
    later(raw.at[pl.ds(0, ZL * (Y - 1))], ys_sem)

    def piece(q, block):
        return raw.at[block, pl.ds(q * ROWS, ROWS)]

    def along_y(q, block, far):
        part = piece(q, block)
        for peer in y_peers:
            remote(part, part, ys_sem, yr_sem.at[q, far], at_cells(peer, zl)).start()

    def along_z(q, block, m, slot):
        part = piece(q, block)
        remote(
            part, part, zs_sem, zr_sem.at[q, slot - 1], at_cells(y, z_peer[m])
        ).start()

    def from_z(q, m):
        block = y * ZL + z_peer[m]
        part = piece(q, block)
        remote(part, part, zs_sem, zr_sem.at[q, m - 1], opposite).wait_recv()
        return block

    for q in range(CHUNKS):
        along_z(q, cell, 4, 4)
    for q in range(CHUNKS):
        for m in (1, 2, 3):
            along_z(q, cell, m, m)
        along_y(q, cell, 0)

    for copy in loads[:4]:
        copy.wait()
    top = lax.Precision.HIGHEST
    scale8 = jnp.broadcast_to(scale_v[...], (8, 52))
    eye = (iota((64, 52), 0) == iota((64, 52), 1)).astype(F32)
    scale_row = dot_nt(scale8, eye, top)
    scale_col = dot_nt(eye, scale8, top)
    lag = jnp.abs(iota((64, 64), 0) - iota((64, 64), 1))
    decay = jnp.exp(lag.astype(F32) * (-1.0 / 6.0))
    table = jnp.where(lag <= band_s[0, 0], decay, 0.0)
    table = table * scale_col[:, 0:1] * scale_row[0:1, :]
    first = sw_v[...]
    weeks = jnp.concatenate([first + a for a in range(4)], axis=1)
    source_pick = (iota((64, 512), 0) == weeks).astype(F32)
    source_rows = dot_nn(table, source_pick, top)
    row_hi = source_rows.astype(BF16)
    rest = source_rows - row_hi.astype(F32)
    row_mid = rest.astype(BF16)
    row_lo = (rest - row_mid.astype(F32)).astype(BF16)
    rows3 = jnp.concatenate([row_hi, row_mid, row_lo], axis=0)
    repeat = ((iota((1024, 256), 0) & 255) == iota((1024, 256), 1)).astype(BF16)
    target_first = jnp.broadcast_to(tw_v[...], (8, 256)).astype(F32).astype(BF16)
    target_col = dot_nt(repeat, target_first)[:, 0:1].astype(I32)
    target_week = target_col + (iota((1024, 1), 0) >> 8)
    target_pick = ((iota((1024, 192), 1) & 63) == target_week).astype(F32).astype(BF16)
    for q in range(CHUNKS):
        weights[q] = dot_nn(target_pick, rows3[:, q * 256 : (q + 1) * 256])
    loads[4].wait()
    for quad in range(2):
        rows = [
            c_buf[(g * 2 + quad) * QUAD * KC : (g * 2 + quad + 1) * QUAD * KC, :].astype(F32)
            for g in range(Y)
        ]
        ct[quad] = jnp.concatenate(rows, axis=0).T.astype(BF16)

    for q in range(CHUNKS):
        for m in (1, 4, 2, 3):
            block = from_z(q, m)
            if m == 4:
                for near in (1, 2, 3):
                    along_z(q, block, near, near + 4)
            along_y(q, block, m // 4)
    loads[5].wait()
    targets = g3[...].reshape(4 * TARGETS, COLS)
    offset = iota((TARGETS, 4 * TARGETS), 1) - 4 * iota((TARGETS, 4 * TARGETS), 0)
    for k in range(4):
        g2[k * TARGETS : (k + 1) * TARGETS] = dot_nn(
            (offset == k).astype(F32).astype(BF16), targets
        ).astype(BF16)

    for q in range(CHUNKS):
        for m in (5, 6, 7):
            along_y(q, from_z(q, m), 1)

    mine = (iota((8, 512), 1) & 127) == iota((8, 512), 0) + snd * 8
    mine = mine.astype(F32)
    wide = (source_rows[:52].reshape(52, 1, 512) * mine.reshape(1, 8, 512)).reshape(416, 512)
    wide_hi = wide.astype(BF16)
    wide_lo = (wide - wide_hi.astype(F32)).astype(BF16)
    for q in range(CHUNKS):
        spread[0, q] = wide_hi[:, q * 256 : (q + 1) * 256]
        spread[1, q] = wide_lo[:, q * 256 : (q + 1) * 256]

    def unpack(q, quad):
        blocks = [
            raw[pl.ds((g * 2 + quad) * QUAD, QUAD), q * ROWS : (q + 1) * ROWS].astype(F32)
            for g in range(Y)
        ]
        halves = [
            jnp.concatenate(
                [b[:, a * KC : (a + 1) * KC, :].reshape(QUAD * KC, 128) for b in blocks], axis=0
            ).astype(BF16)
            for a in range(2)
        ]
        return jnp.concatenate(halves, axis=1)

    own_quad = zl // QUAD

    def from_y(q, far):
        part = raw.at[pl.ds(0, QUAD * (Y - 1)), pl.ds(0, ROWS)]
        remote(part, part, ys_sem, yr_sem.at[q, far], opposite).wait_recv()

    def near_flux(q):
        from_y(q, 0)
        total = dot_nn(ct[own_quad], unpack(q, own_quad))
        for c in range(2):
            acc[q, c] = total[:, c * 128 : (c + 1) * 128]

    def partial_flux(q):
        from_y(q, 1)
        total = jnp.concatenate([acc[q, 0], acc[q, 1]], axis=1)
        total = total + dot_nn(ct[1 - own_quad], unpack(q, 1 - own_quad))
        for c in range(2):
            half = total[:, c * 128 : (c + 1) * 128]
            acc[q, c] = half
            sum_out[q, c] = half.astype(BF16).reshape(X, SHARD, 128)
        for h in range(2):
            p = 2 * q + h
            later(sum_in.at[p], ss_sem.at[p])
            for n, (xx, cc) in enumerate(sum_peers):
                remote(
                    sum_out.at[q, cc, xx, pl.ds(h * HALF, HALF)], sum_in.at[p, n],
                    ss_sem.at[p], sr_sem.at[p], at_snd(xx, zh, cc),
                ).start()

    def across_z(q, h):
        p = 2 * q + h
        every = sum_in.at[p]
        remote(every, every, ss_sem.at[p], sr_sem.at[p], opposite).wait_recv()
        rows = pl.ds(pl.multiple_of(x * SHARD + h * HALF, HALF), HALF)
        own = acc[q, core, rows, :] + jnp.sum(sum_in[p].astype(F32), axis=0)
        z_own[p] = own
        z_out[p] = own.astype(BF16)
        copy = remote(z_out.at[p], z_in.at[p], hs_sem.at[p], hr_sem.at[p], opposite)
        copy.start()
        drains.append(copy.wait_send)
        return copy

    def share(q, h, copy):
        p = 2 * q + h
        copy.wait_recv()
        flux[q, core, x, h * HALF : (h + 1) * HALF] = (z_own[p] + z_in[p].astype(F32)).astype(BF16)
        part = flux.at[q, core, x, pl.ds(h * HALF, HALF)]
        later(sum_in.at[p], gs_sem.at[p])
        for xx, cc in sum_peers:
            remote(part, part, gs_sem.at[p], gr_sem.at[p], at_snd(xx, zh, cc)).start()

    def whole_flux(q):
        return jnp.concatenate([flux[q, c].reshape(COLS, 128) for c in range(2)], axis=1)

    def products(q):
        for h in range(2):
            p = 2 * q + h
            every = sum_in.at[p]
            remote(every, every, gs_sem.at[p], gr_sem.at[p], opposite).wait_recv()
        both = dot_nn(g2[...], whole_flux(q)) * weights[q]
        both = both[:, :128] + both[:, 128:]
        return jnp.sum(both.reshape(4, TARGETS, 128), axis=0)

    for q in range(CHUNKS):
        near_flux(q)
    for q in range(CHUNKS):
        partial_flux(q)
    pl.semaphore_wait(token, 1)
    moved = [across_z(q, h) for q, h in PIECES]
    for q, h in PIECES:
        share(q, h, moved[2 * q + h])
    pair_x[...] = products(0)
    total = (pair_x[...] + products(1)).reshape(CELLS, 8, 128)
    pair_x[...] = total.reshape(TARGETS, 128)
    pair_out[...] = total.astype(BF16)

    later(pair_in, ps_sem)
    for d in (2, 1, 3, 0):
        for m in FAR_FIRST + (0,):
            if m or d:
                target = ((y + d) % Y) * ZL + (z_peer[m] if m else zl)
                remote(
                    pair_out.at[target], pair_in.at[m * Y + d - 1], ps_sem, pr_sem, (target, snd)
                ).start()

    hq = jnp.zeros((416, COLS), F32)
    for q in range(CHUNKS):
        columns = whole_flux(q)
        hq = hq + dot_nt(spread[0, q], columns) + dot_nt(spread[1, q], columns)
    hq_ref[...] = hq.astype(BF16)

    remote(pair_in, pair_in, ps_sem, pr_sem, opposite).wait_recv()
    own = pair_x[pl.ds(pl.multiple_of(cell * 8, 8), 8), :]
    pc_ref[...] = own + jnp.sum(pair_in[...].astype(F32), axis=0)

    finish()


def shards(
    footprint, spatial_cov, week_scale, band_width, sounding_weeks, target_print, target_weeks,
):
    hbm = pl.BlockSpec(memory_space=pltpu.HBM)
    vmem = pl.BlockSpec(memory_space=pltpu.VMEM)
    dma = pltpu.SemaphoreType.DMA
    hq, pair = pl.pallas_call(
        kernel,
        out_shape=(
            jax.ShapeDtypeStruct((416, COLS), BF16),
            jax.ShapeDtypeStruct((8, 128), F32),
        ),
        in_specs=[hbm] * 4 + [pl.BlockSpec(memory_space=pl.ANY)] + [hbm] * 2,
        out_specs=(vmem, vmem),
        scratch_shapes=[
            pltpu.VMEM((CELLS, 4 * KC, 128), BF16),
            pltpu.VMEM((768, COLS), BF16),
            pltpu.VMEM((2, COLS, GROUP), BF16),
            pltpu.VMEM((256, 4, COLS), BF16),
            pltpu.VMEM((1024, COLS), BF16),
            pltpu.VMEM((1, 52), F32),
            pltpu.VMEM((1, 128), I32),
            pltpu.VMEM((1, 256), I32),
            pltpu.SMEM((1, 1), I32),
            pltpu.VMEM((CHUNKS, 1024, 256), F32),
            pltpu.VMEM((2, CHUNKS, 416, 256), BF16),
            pltpu.VMEM((CHUNKS, 2, COLS, 128), F32),
            pltpu.VMEM((CHUNKS, 2, X, SHARD, 128), BF16),
            pltpu.VMEM((len(PIECES), 2 * X - 1, HALF, 128), BF16),
            pltpu.VMEM((len(PIECES), HALF, 128), BF16),
            pltpu.VMEM((len(PIECES), HALF, 128), BF16),
            pltpu.VMEM((len(PIECES), HALF, 128), F32),
            pltpu.VMEM((CHUNKS, 2, X, SHARD, 128), BF16),
            pltpu.VMEM((TARGETS, 128), F32),
            pltpu.VMEM((CELLS, 8, 128), BF16),
            pltpu.VMEM((CELLS - 1, 8, 128), BF16),
            dma((7,)),
            dma, dma((CHUNKS, ZL - 1)),
            dma, dma((CHUNKS, 2)),
            dma((len(PIECES),)), dma((len(PIECES),)),
            dma((len(PIECES),)), dma((len(PIECES),)),
            dma((len(PIECES),)), dma((len(PIECES),)),
            dma, dma,
            pltpu.SemaphoreType.REGULAR,
        ],
        compiler_params=pltpu.CompilerParams(
            collective_id=0, has_side_effects=True, vmem_limit_bytes=48 << 20
        ),
        name="prior_products",
    )(
        in_hbm(jnp.transpose(footprint, (1, 2, 0)).reshape(4 * KC, 128)),
        in_hbm(spatial_cov),
        in_hbm(target_print),
        in_hbm(week_scale.reshape(1, 52)),
        band_width.reshape(1, 1),
        in_hbm(sounding_weeks.reshape(1, 128)),
        in_hbm(target_weeks.reshape(1, 256)),
    )
    return jnp.transpose(hq.reshape(52, 8, COLS), (1, 0, 2)), pair.T


def solution(mesh):
    placed = (
        P(None, None, ("snd", "cells")),
        P("snd", "cells"),
        P(),
        P(),
        P(),
        P("snd", None, "cells"),
        P("snd"),
    )
    return jax.shard_map(
        shards,
        mesh=mesh,
        in_specs=placed,
        out_specs=(P("snd", None, "cells"), P(None, ("snd", "cells"))),
        check_vma=False,
    )
```
